256 devices in a mesh: clus: 16 (over z, core), ang: 16 (over x, y).
Axes of the slice: x: 4, y: 4, z: 8, core: 2. Of those that a mesh axis runs over, the one named last changes fastest.
Arguments:
- child_pattern: float32 [512, 2, 128, 64], P('clus', None, 'ang'), may hold values from -6 to 6
- child_sources: int32 [512, 189], replicated, may hold values from 0 to 511
- child_classes: int32 [512, 189], replicated, may hold values from 0 to 315
- child_counts: int32 [512], replicated, may hold values from 1 to 189, as said below
- parent_sources: int32 [64, 189], replicated, may hold values from 0 to 63
- parent_classes: int32 [64, 189], replicated, may hold values from 0 to 315
- parent_counts: int32 [64], replicated, may hold values from 1 to 189, as said below
- child_table: float32 [316, 2, 128, 64], P(None, None, 'ang'), may hold values from -0.4375 to 0.4375
- parent_table: float32 [316, 2, 256, 128], P(None, None, 'ang'), may hold values from -0.15625 to 0.15625
- theta_index: int32 [128, 4], replicated, may hold values from 0 to 63, as said below
- theta_weight: float32 [128, 4], replicated, as said below
- phi_index: int32 [256, 4], P('ang'), may hold values from 0 to 127, as said below
- phi_weight: float32 [256, 4], P('ang'), as said below
- shift_angle: float32 [8, 256, 128], P(None, 'ang'), may hold values from -3.140625 to 3.140625
Outputs:
- child_incoming: float32 [512, 2, 128, 64], P('clus', None, 'ang')
- parent_pattern: float32 [64, 2, 256, 128], P('clus', None, 'ang')
- parent_incoming: float32 [64, 2, 256, 128], P('clus', None, 'ang')
The draws below stay inside these ranges and needn't reach their ends.
Inputs may be any that keep to these rules, and one draw needn't show every extreme that they name: `child_counts`: the number of live slots of each child far list; slots beyond it are padding. `parent_counts`: the number of live slots of each parent far list; slots beyond it are padding. `theta_index`: row i holds four consecutive child rows beginning at min(max(i // 2 - 2 or i // 2 - 1, 0), 60). `phi_index`: row j holds four cyclically consecutive child columns beginning at j // 2 - 2 or j // 2 - 1, modulo 128. `theta_weight`: lagrange weights of four equispaced nodes. `phi_weight`: lagrange weights of four equispaced nodes.
All inputs are finite; a program needn't handle non-finite values.
Results may differ from the reference program's by a relative error of at most 0.00007.
Values sent between devices are 32-bit elements; how exact they have to be, the bound alone decides.
A program may use at most 64 MiB of HBM per device.

```python
import jax
import jax.numpy as jnp
from jax import lax

C1D = 32
MFAR = 189
CLASSES = 316
TH1 = 64
PH1 = 128
TH2 = 128
PH2 = 256
C1 = 512
C2 = 64


def counts_law(key, total_rows, group_rows):
    first_key, second_key, third_key = jax.random.split(key, 3)
    group_total = total_rows // group_rows
    levels = jax.random.randint(first_key, (group_total,), 2, 9)
    ceiling = jnp.maximum(MFAR * levels // 8, 1)
    ceiling_rows = jnp.repeat(ceiling, group_rows)
    counts = jax.random.randint(second_key, (total_rows,), 0, MFAR) % ceiling_rows + 1
    chosen = jax.random.randint(third_key, (), 0, total_rows)
    return counts.at[chosen].set(MFAR).astype(jnp.int32)


def lagrange_law(key, total_rows):
    offset = jax.random.uniform(key, (total_rows,), jnp.float32, 0.2, 0.8)
    first = -offset * (offset - 1.0) * (offset - 2.0) / 6.0
    second = (offset + 1.0) * (offset - 1.0) * (offset - 2.0) / 2.0
    third = -(offset + 1.0) * offset * (offset - 2.0) / 2.0
    fourth = (offset + 1.0) * offset * (offset - 1.0) / 6.0
    return jnp.stack([first, second, third, fourth], 1).astype(jnp.float32)


def draw_child_counts(key, part):
    key = jax.random.fold_in(key, 1)
    return counts_law(key, C1, C1D)


def draw_parent_counts(key, part):
    key = jax.random.fold_in(key, 2)
    return counts_law(key, C2, C1D // 8)


def draw_theta_index(key, part):
    key = jax.random.fold_in(key, 3)
    rows_here = jnp.arange(TH2, dtype=jnp.int32)
    shifts = jax.random.randint(key, (TH2,), -2, 0)
    begin = jnp.clip(rows_here // 2 + shifts, 0, TH1 - 4)
    return (begin[:, None] + jnp.arange(4, dtype=jnp.int32)[None, :]).astype(jnp.int32)


def draw_phi_index(key, part):
    key = jax.random.fold_in(key, 4)
    cols_here = jnp.arange(PH2, dtype=jnp.int32)
    shifts = jax.random.randint(key, (PH2,), -2, 0)
    begin = cols_here // 2 + shifts
    return ((begin[:, None] + jnp.arange(4, dtype=jnp.int32)[None, :]) % PH1).astype(jnp.int32)


def draw_theta_weight(key, part):
    key = jax.random.fold_in(key, 5)
    return lagrange_law(key, TH2)


def draw_phi_weight(key, part):
    key = jax.random.fold_in(key, 6)
    return lagrange_law(key, PH2)


def set_ends(drawn, key, smallest, largest):
    spot = [jax.random.randint(jax.random.fold_in(key, axis), (), 0, length) for axis, length in enumerate(drawn.shape)]
    longest = drawn.shape.index(max(drawn.shape))
    next_to = spot[:longest] + [(spot[longest] + 1) % drawn.shape[longest]] + spot[longest + 1:]
    return drawn.at[tuple(spot)].set(smallest).at[tuple(next_to)].set(largest)


def steps_of(rng, dims, cuts, least, high):
    loudness = 1.0
    for position, parts in cuts:
        heights = jax.random.uniform(jax.random.fold_in(jax.random.fold_in(rng, 6), position), (parts,), jnp.float32, least / len(cuts), high / len(cuts))
        loudness = loudness * jnp.repeat(jnp.exp(heights), dims[position] // parts).reshape((-1,) + (1,) * (len(dims) - 1 - position))
    return loudness


def centred(own_key, extent, scale, reach, cuts=(), held_as=jnp.bfloat16):
    level = steps_of(own_key, extent, cuts, -0.22, 0.18) if cuts else 1.0
    entries = jax.random.normal(own_key, extent, jnp.float32) * scale * level
    return jnp.minimum(jnp.maximum(entries, -reach), reach).astype(held_as)


def setup_inputs(seed: int = 0) -> dict:
    keys = jax.random.split(jax.random.key(seed), 15)
    return {
        "child_pattern": centred(keys[0], (C1, 2, PH1, TH1), 1.0, 6.0, ((0, 16), (2, 16)), jnp.float32),
        "child_sources": set_ends(jax.random.randint(keys[1], (C1, MFAR), 0, C1), jax.random.fold_in(keys[1], 1), 0, C1 - 1).astype(jnp.int32),
        "child_classes": set_ends(jax.random.randint(keys[2], (C1, MFAR), 0, CLASSES), jax.random.fold_in(keys[2], 1), 0, CLASSES - 1).astype(jnp.int32),
        "child_counts": draw_child_counts(jax.random.fold_in(keys[14], 71), 0),
        "parent_sources": set_ends(jax.random.randint(keys[4], (C2, MFAR), 0, C2), jax.random.fold_in(keys[4], 1), 0, C2 - 1).astype(jnp.int32),
        "parent_classes": set_ends(jax.random.randint(keys[5], (C2, MFAR), 0, CLASSES), jax.random.fold_in(keys[5], 1), 0, CLASSES - 1).astype(jnp.int32),
        "parent_counts": draw_parent_counts(jax.random.fold_in(keys[14], 71), 0),
        "child_table": centred(keys[7], (CLASSES, 2, PH1, TH1), MFAR ** -0.5, 0.4375, ((2, 16),), jnp.float32),
        "parent_table": centred(keys[8], (CLASSES, 2, PH2, TH2), (8 * MFAR) ** -0.5, 0.15625, ((2, 16),), jnp.float32),
        "theta_index": draw_theta_index(jax.random.fold_in(keys[14], 71), 0),
        "theta_weight": draw_theta_weight(jax.random.fold_in(keys[14], 71), 0),
        "phi_index": draw_phi_index(jax.random.fold_in(keys[14], 71), 0),
        "phi_weight": draw_phi_weight(jax.random.fold_in(keys[14], 71), 0),
        "shift_angle": jnp.clip(jax.random.uniform(keys[13], (8, PH2, TH2), jnp.float32, -3.140625, 3.140625), -3.140625, 3.140625),
    }


def translate(pattern, source_ids, class_ids, live_counts, table):
    dest_count = source_ids.shape[0]
    flat_pattern = pattern.reshape(pattern.shape[0], 2, -1)
    flat_table = table.reshape(table.shape[0], 2, -1)
    initial = jnp.zeros((dest_count, 2, flat_pattern.shape[2]), jnp.float32)

    def add_slot(slot_index, total):
        source_vals = flat_pattern[source_ids[:, slot_index]]
        factor = flat_table[class_ids[:, slot_index]]
        real_part = source_vals[:, 0] * factor[:, 0] - source_vals[:, 1] * factor[:, 1]
        imag_part = source_vals[:, 0] * factor[:, 1] + source_vals[:, 1] * factor[:, 0]
        live = (slot_index < live_counts)[:, None, None]
        return total + jnp.where(live, jnp.stack([real_part, imag_part], 1), 0.0)

    total = lax.fori_loop(0, MFAR, add_slot, initial)
    return total.reshape((dest_count,) + pattern.shape[1:])


def stencil_matrix(index_table, weight_table, width):
    columns = jnp.arange(width, dtype=jnp.int32)
    hits = (index_table[:, :, None] == columns[None, None, :])
    return jnp.sum(jnp.where(hits, weight_table[:, :, None], 0.0), axis=1)


def reference(child_pattern, child_sources, child_classes, child_counts, parent_sources, parent_classes, parent_counts, child_table, parent_table, theta_index, theta_weight, phi_index, phi_weight, shift_angle):
    child_incoming = translate(child_pattern, child_sources, child_classes, child_counts, child_table)
    theta_matrix = stencil_matrix(theta_index, theta_weight, TH1)
    phi_matrix = stencil_matrix(phi_index, phi_weight, PH1)
    polar = jnp.einsum("cqpt,it->cqpi", child_pattern, theta_matrix, precision=lax.Precision.HIGHEST)
    interpolated = jnp.einsum("cqpi,jp->cqji", polar, phi_matrix, precision=lax.Precision.HIGHEST)
    grouped = interpolated.reshape(C2, 8, 2, PH2, TH2)
    cosine = jnp.cos(shift_angle)[None]
    sine = jnp.sin(shift_angle)[None]
    real_part = jnp.sum(grouped[:, :, 0] * cosine - grouped[:, :, 1] * sine, axis=1)
    imag_part = jnp.sum(grouped[:, :, 0] * sine + grouped[:, :, 1] * cosine, axis=1)
    parent_pattern = jnp.stack([real_part, imag_part], 1)
    parent_incoming = translate(parent_pattern, parent_sources, parent_classes, parent_counts, parent_table)
    return child_incoming, parent_pattern, parent_incoming
```

```python
import functools

import jax
import jax.numpy as jnp
from jax import lax
from jax.experimental import pallas as pl
from jax.experimental.pallas import tpu as pltpu
from jax.sharding import PartitionSpec as P

MESH = pl.DeviceIdType.MESH
SLOTS = 189
CLASSES = 316
HEAD = 96
TAIL = 32
CHUNKS = 2
CHILD_STEPS = -(-(SLOTS - HEAD) // TAIL)
PARENT_STEPS = -(-SLOTS // TAIL)
CHILD_ROWS = 32 * CHILD_STEPS
PARENT_ROWS = 8 * PARENT_STEPS


def rows_at(start, size):
    return pl.ds(pl.multiple_of(start, 8), size)


def gather_kernel(
    pat_hbm, cs_hbm, cc_hbm, ccnt_hbm, ps_hbm, pc_hbm, pcnt_hbm, tab_hbm,
    thi_hbm, thw_hbm, phi_hbm, phw_hbm, ang_hbm,
    g_ref, f_ref, acc_ref, pg_ref, ci_ref, pi_ref,
    pat, sv, cv, ccnt, psv, pcv, pcnt, tab, thi, thw, phi, phw, ang,
    own, hs, hr, zs, ta, sa_s, sa_c,
    loc, smsem, hsend, hrecv, csend, crecv, cssend, csrecv, psend, precv, pssend, psrecv,
):
    r = lax.axis_index("clus")
    a = lax.axis_index("ang")
    sib = r + 1 - 2 * lax.rem(r, 2)
    up, down = lax.rem(r + 2, 16), lax.rem(r + 14, 16)
    ahead, behind = lax.rem(a + 1, 16), lax.rem(a + 15, 16)

    lane_block = pl.ds(pl.multiple_of(lax.div(r, 4) * 128, 128), 128)
    row_block = rows_at(lax.div(r, 2) * 8, 8)
    locals_ = [
        (pat_hbm, pat),
        (cs_hbm.at[:, lane_block], sv),
        (cc_hbm.at[:, lane_block], cv),
        (ccnt_hbm, ccnt),
        (ps_hbm.at[row_block, :], psv),
        (pc_hbm.at[row_block, :], pcv),
        (pcnt_hbm, pcnt),
        (thi_hbm, thi),
        (thw_hbm, thw),
        (phi_hbm, phi),
        (phw_hbm, phw),
        (ang_hbm, ang),
        (tab_hbm, tab),
    ]
    copies = [pltpu.make_async_copy(src, dst, loc.at[i]) for i, (src, dst) in enumerate(locals_)]
    for copy in copies:
        copy.start()

    barrier = pltpu.get_barrier_semaphore()
    for target in (up, down, sib):
        pl.semaphore_signal(barrier, inc=1, device_id={"clus": target}, device_id_type=MESH)
    for target in (ahead, behind):
        pl.semaphore_signal(barrier, inc=1, device_id={"ang": target}, device_id_type=MESH)
    pl.semaphore_wait(barrier, 5)

    def mover(buffer, block_rows, send, recv, sib_send, sib_recv):
        size = block_rows // CHUNKS

        def part(owner, ch):
            return buffer.at[rows_at(owner * block_rows + ch * size, size), :]

        def ring(way, step, ch):
            back = 16 - 2 * (step - 1) if way == 0 else 2 * (step - 1)
            block = part(lax.rem(r + back, 16), ch)
            k = (8 - step) if way == 0 else step
            return pltpu.make_async_remote_copy(
                src_ref=block, dst_ref=block,
                send_sem=send.at[way, step - 1, ch], recv_sem=recv.at[k, ch],
                device_id={"clus": up if way == 0 else down}, device_id_type=MESH,
            )

        def arrived(way, step, ch):
            k = (8 - step) if way == 0 else step
            block = part(lax.rem(r + 2 * k, 16), ch)
            pltpu.make_async_remote_copy(
                src_ref=block, dst_ref=block,
                send_sem=send.at[way, step - 1, ch], recv_sem=recv.at[k, ch],
                device_id={"clus": up if way == 0 else down}, device_id_type=MESH,
            ).wait_recv()

        def side(k, ch, mine=True):
            block = part(lax.rem((r if mine else sib) + 2 * k, 16), ch)
            return pltpu.make_async_remote_copy(
                src_ref=block, dst_ref=block,
                send_sem=sib_send.at[k, ch], recv_sem=sib_recv.at[k, ch],
                device_id={"clus": sib}, device_id_type=MESH,
            )

        def uses(way, step, ch):
            return step < 4 or (ch < CHUNKS // 2) == (way == 0)

        def first(ch):
            for way in (0, 1):
                ring(way, 1, ch).start()
            side(0, ch).start()

        def onward(step, ch):
            for way in (0, 1):
                if uses(way, step, ch):
                    arrived(way, step, ch)
                    if step < 4 and uses(way, step + 1, ch):
                        ring(way, step + 1, ch).start()
                    side((8 - step) if way == 0 else step, ch).start()

        def landed():
            for k in range(8):
                for ch in range(CHUNKS):
                    side(k, ch, mine=False).wait_recv()

        def drained():
            for ch in range(CHUNKS):
                for step in range(1, 5):
                    for way in (0, 1):
                        if uses(way, step, ch):
                            ring(way, step, ch).wait_send()
                for k in range(8):
                    side(k, ch).wait_send()

        return first, onward, landed, drained

    c_first, c_onward, c_landed, c_drained = mover(g_ref, 256, csend, crecv, cssend, csrecv)
    p_first, p_onward, p_landed, p_drained = mover(pg_ref, 128, psend, precv, pssend, psrecv)

    copies[0].wait()
    size = 32 // CHUNKS
    for ch in range(CHUNKS):
        x = pat[ch * size:(ch + 1) * size]
        x = jnp.concatenate([x[:, 0], x[:, 1]], axis=2).reshape(size * 8, 128)
        own[ch * size * 8:(ch + 1) * size * 8, :] = x
        g_ref[rows_at(r * 256 + ch * size * 8, size * 8), :] = x
        c_first(ch)

    halo = []
    for way in (0, 1):
        for j in range(2):
            hs[way, j * 32:(j + 1) * 32, :] = own[pl.ds((6 if way == 0 else 0) + j, 32, stride=8), :]
        copy = pltpu.make_async_remote_copy(
            src_ref=hs.at[way], dst_ref=hr.at[way], send_sem=hsend.at[way], recv_sem=hrecv.at[way],
            device_id={"ang": ahead if way == 0 else behind}, device_id_type=MESH,
        )
        copy.start()
        halo.append(copy)

    for i in (1, 2, 3):
        copies[i].wait()
    count_row = ccnt[pl.ds(lax.div(r, 4), 1), :]
    own_rows = rows_at(lax.rem(r, 4) * 32, 32)
    slot = lax.broadcasted_iota(jnp.int32, (128, 128), 0)

    def lists(start, stop):
        s, c = sv[start:stop, :], cv[start:stop, :]
        live = slot[:stop - start] + start < count_row
        s = jnp.where(live, s, 0) * 8
        c = jnp.where(live, c, CLASSES) * 16
        return s, c

    s, c = lists(0, 128)
    ta[0] = lax.shift_right_logical(s, 3).T
    ta[1] = lax.shift_right_logical(c, 4).T
    fill = [
        pltpu.make_async_copy(ta.at[0, own_rows, :], sa_s, smsem.at[0]),
        pltpu.make_async_copy(ta.at[1, own_rows, :], sa_c, smsem.at[1]),
    ]
    for copy in fill:
        copy.start()

    c_onward(1, 0)

    s, c = lists(HEAD, SLOTS)
    rest = 128 - (SLOTS - HEAD)
    s = jnp.concatenate([s, jnp.zeros((rest, 128), jnp.int32)], axis=0)
    c = jnp.concatenate([c, jnp.full((rest, 128), CLASSES * 16, jnp.int32)], axis=0)
    c = jnp.where(slot == 127, count_row, c)
    ta[2] = s.T
    ta[3] = c.T
    ts, tc = ta[2, own_rows, :], ta[3, own_rows, :]
    for i in range(CHILD_STEPS):
        ci_ref[i * 32:(i + 1) * 32, :] = pltpu.roll(ts, (128 - i * TAIL) % 128, 1) if i else ts
        ci_ref[CHILD_ROWS + i * 32:CHILD_ROWS + (i + 1) * 32, :] = (
            pltpu.roll(tc, (128 - i * TAIL) % 128, 1) if i else tc
        )

    for i in (4, 5, 6):
        copies[i].wait()
    line = lax.broadcasted_iota(jnp.int32, (8, 128), 0)
    lane = lax.broadcasted_iota(jnp.int32, (8, 128), 1)
    counts = jnp.zeros((8, 128), jnp.int32)
    for i in range(8):
        counts = jnp.where(line == i, pcnt[lax.div(r, 2) * 8 + i], counts)
    pads = jnp.zeros((8, 256 - SLOTS), jnp.int32)
    for half in range(2):
        if half == 0:
            s, c = psv[:, :128], pcv[:, :128]
        else:
            s = jnp.concatenate([psv[:, 128:], pads], axis=1)
            c = jnp.concatenate([pcv[:, 128:], pads], axis=1)
        live = lane + half * 128 < counts
        s = jnp.where(live, s, 64) * 32
        c = jnp.where(live, c, 0) * 32
        for i in range(half * 128 // TAIL, min((half + 1) * 128 // TAIL, PARENT_STEPS)):
            turn = (128 - (i * TAIL - half * 128)) % 128
            si = pltpu.roll(s, turn, 1) if turn else s
            cj = pltpu.roll(c, turn, 1) if turn else c
            pi_ref[i * 8:(i + 1) * 8, :] = si
            pi_ref[PARENT_ROWS + i * 8:PARENT_ROWS + (i + 1) * 8, :] = jnp.where(lane == 127, counts, cj)
    pg_ref[2048:2080, :] = jnp.zeros((32, 128), jnp.float32)

    c_onward(1, 1)

    copies[12].wait()

    def operators(col):
        for b in range(3):
            lo, hi = b * 128, min((b + 1) * 128, CLASSES)
            x = jnp.concatenate([tab[0, col, :, lo:hi], tab[1, col, :, lo:hi]], axis=0)
            if hi - lo < 128:
                x = jnp.concatenate([x, jnp.zeros((128, 128 - (hi - lo)), jnp.float32)], axis=1)
            y = x.T
            f_ref[pl.ds(lo * 16 + col, 128, stride=16), :] = y
            f_ref[pl.ds(lo * 16 + col + 8, 128, stride=16), :] = pltpu.roll(y, 64, 1)

    for col in range(4):
        operators(col)
    c_onward(2, 0)
    for col in range(4, 8):
        operators(col)
    c_onward(2, 1)

    for i in (7, 8, 9, 10, 11):
        copies[i].wait()
    for copy in halo:
        copy.wait_recv()
    offset = lax.rem(phi[...] - a * 8 + (2 + 128), 128)
    weights = phw[...]
    base = lax.shift_right_logical(lax.broadcasted_iota(jnp.int32, (1, 16), 1), 1)
    taps = []
    for d in range(5):
        tap = jnp.zeros((1, 16), jnp.float32)
        for i in range(4):
            tap = tap + jnp.where(offset[i:i + 1, :] == base + d, weights[i:i + 1, :], 0.0)
        taps.append(tap)
    cols = [hr[0, :32, :], hr[0, 32:, :]]
    cols += [own[pl.ds(j, 32, stride=8), :] for j in range(8)]
    cols += [hr[1, :32, :], hr[1, 32:, :]]
    for j in range(16):
        z = jnp.zeros((32, 128), jnp.float32)
        for d in range(5):
            z = z + taps[d][:, j:j + 1] * cols[j // 2 + d]
        zs[pl.ds(j, 32, stride=16), :] = z

    c_onward(3, 0)

    row = lax.broadcasted_iota(jnp.int32, (64, 128), 0)
    theta = jnp.zeros((64, 128), jnp.float32)
    for i in range(4):
        theta = theta + jnp.where(thi[i:i + 1, :] == row, thw[i:i + 1, :], 0.0)
    blank = jnp.zeros((64, 128), jnp.float32)
    pair = jnp.concatenate(
        [jnp.concatenate([theta, blank], axis=1), jnp.concatenate([blank, theta], axis=1)], axis=0
    )
    angles = ang[...]
    cosine, sine = jnp.cos(angles), jnp.sin(angles)

    c_onward(3, 1)

    for parent in range(4):
        y = jnp.dot(
            zs[parent * 128:(parent + 1) * 128, :], pair,
            precision=lax.Precision.HIGHEST, preferred_element_type=jnp.float32,
        )
        re = y[:, :128] * cosine - y[:, 128:] * sine
        im = y[:, :128] * sine + y[:, 128:] * cosine
        re = jnp.sum(re.reshape(8, 16, 128), axis=0)
        im = jnp.sum(im.reshape(8, 16, 128), axis=0)
        pg_ref[rows_at(r * 128 + parent * 32, 16), :] = re
        pg_ref[rows_at(r * 128 + parent * 32 + 16, 16), :] = im
        if parent % 2:
            p_first(parent // 2)

    for ch in range(CHUNKS):
        c_onward(4, ch)
    for copy in fill:
        copy.wait()
    c_landed()

    events = {}
    for i, (step, ch) in enumerate([(s, h) for s in range(1, 5) for h in range(CHUNKS)]):
        events.setdefault(min(2 + 4 * i, 31), []).append(functools.partial(p_onward, step, ch))

    g3, f4 = g_ref.reshape(512, 8, 128), f_ref.reshape(384, 2, 8, 128)

    def head(p, carry):
        zero = jnp.zeros((8, 128), jnp.float32)
        one, two = zero, zero
        for m in range(HEAD):
            s, c = sa_s[p, m], sa_c[p, m]
            x = g3[s]
            one = one + x * f4[c, 0]
            two = two + x * f4[c, 1]
        acc_ref[rows_at(p * 16, 8), :] = one
        acc_ref[rows_at(p * 16 + 8, 8), :] = two
        for at, todo in events.items():
            @pl.when(p == at)
            def _():
                for go in todo:
                    go()
        return carry

    lax.fori_loop(0, 32, head, 0)

    p_landed()
    for copy in halo:
        copy.wait_send()
    c_drained()
    p_drained()


def list_kernel(
    g_ref, f_ref, acc_ref, pg_ref, ci_ref, pi_ref, pt_ref,
    child_out, pattern_out, incoming_out,
    ci, pi, child, incoming, sem,
):
    r = lax.axis_index("clus")
    fill_p = pltpu.make_async_copy(pi_ref, pi, sem.at[0])
    fill_c = pltpu.make_async_copy(ci_ref, ci, sem.at[1])
    fill_p.start()
    fill_c.start()
    pattern = pltpu.make_async_copy(pg_ref.at[rows_at(r * 128, 128), :], pattern_out, sem.at[2])
    pattern.start()
    fill_p.wait()

    def parent(p, carry):
        line = lax.rem(r, 2) * 4 + p
        steps = lax.div(pi[PARENT_ROWS + line, 127] + (TAIL - 1), TAIL)

        def step(i, total):
            re, im = total
            for m in range(TAIL):
                s = pl.multiple_of(pi[i * 8 + line, m], 32)
                c = pl.multiple_of(pi[PARENT_ROWS + i * 8 + line, m], 32)
                sr, si = pg_ref[pl.ds(s, 16), :], pg_ref[pl.ds(s + 16, 16), :]
                tr, ti = pt_ref[pl.ds(c, 16), :], pt_ref[pl.ds(c + 16, 16), :]
                re = re + (sr * tr - si * ti)
                im = im + (sr * ti + si * tr)
            return re, im

        zero = jnp.zeros((16, 128), jnp.float32)
        re, im = lax.fori_loop(0, steps, step, (zero, zero))
        incoming[rows_at(p * 32, 16), :] = re
        incoming[rows_at(p * 32 + 16, 16), :] = im
        return carry

    lax.fori_loop(0, 4, parent, 0)
    done = pltpu.make_async_copy(incoming, incoming_out, sem.at[3])
    done.start()
    fill_c.wait()

    def tail(p, carry):
        more = jnp.maximum(ci[CHILD_ROWS + p, 127] - HEAD, 0)
        steps = lax.div(more + (TAIL - 1), TAIL)

        def step(i, total):
            one, two = total
            for m in range(TAIL):
                s = pl.multiple_of(ci[i * 32 + p, m], 8)
                c = pl.multiple_of(ci[CHILD_ROWS + i * 32 + p, m], 16)
                x = g_ref[pl.ds(s, 8), :]
                one = one + x * f_ref[pl.ds(c, 8), :]
                two = two + x * f_ref[pl.ds(c + 8, 8), :]
            return one, two

        start = (acc_ref[rows_at(p * 16, 8), :], acc_ref[rows_at(p * 16 + 8, 8), :])
        one, two = lax.fori_loop(0, steps, step, start)
        child[p, 0] = (one - pltpu.roll(one, 64, 1))[:, :64]
        child[p, 1] = (two + pltpu.roll(two, 64, 1))[:, :64]
        return carry

    lax.fori_loop(0, 32, tail, 0)
    last = pltpu.make_async_copy(child, child_out, sem.at[4])
    last.start()
    pattern.wait()
    done.wait()
    last.wait()


def local(
    child_pattern, child_sources, child_classes, child_counts,
    parent_sources, parent_classes, parent_counts,
    child_table, parent_table, theta_index, theta_weight, phi_index, phi_weight, shift_angle,
):
    f32, i32 = jnp.float32, jnp.int32
    hbm = pl.BlockSpec(memory_space=pltpu.HBM)
    vmem = pl.BlockSpec(memory_space=pltpu.VMEM)
    dma = pltpu.SemaphoreType.DMA
    g, f, acc, pg, ci, pi = pl.pallas_call(
        gather_kernel,
        out_shape=(
            jax.ShapeDtypeStruct((4096, 128), f32),
            jax.ShapeDtypeStruct((6144, 128), f32),
            jax.ShapeDtypeStruct((512, 128), f32),
            jax.ShapeDtypeStruct((2080, 128), f32),
            jax.ShapeDtypeStruct((2 * CHILD_ROWS, 128), i32),
            jax.ShapeDtypeStruct((2 * PARENT_ROWS, 128), i32),
        ),
        in_specs=[hbm] * 13,
        out_specs=(vmem,) * 6,
        scratch_shapes=[
            pltpu.VMEM((32, 2, 8, 64), f32),
            pltpu.VMEM((SLOTS, 128), i32),
            pltpu.VMEM((SLOTS, 128), i32),
            pltpu.VMEM((4, 128), i32),
            pltpu.VMEM((8, SLOTS), i32),
            pltpu.VMEM((8, SLOTS), i32),
            pltpu.SMEM((64,), i32),
            pltpu.VMEM((2, 8, 64, CLASSES), f32),
            pltpu.VMEM((4, 128), i32),
            pltpu.VMEM((4, 128), f32),
            pltpu.VMEM((4, 16), i32),
            pltpu.VMEM((4, 16), f32),
            pltpu.VMEM((128, 128), f32),
            pltpu.VMEM((256, 128), f32),
            pltpu.VMEM((2, 64, 128), f32),
            pltpu.VMEM((2, 64, 128), f32),
            pltpu.VMEM((512, 128), f32),
            pltpu.VMEM((4, 128, 128), i32),
            pltpu.SMEM((32, 128), i32),
            pltpu.SMEM((32, 128), i32),
            dma((13,)),
            dma((2,)),
            dma((2,)),
            dma((2,)),
            dma((2, 4, CHUNKS)),
            dma((8, CHUNKS)),
            dma((8, CHUNKS)),
            dma((8, CHUNKS)),
            dma((2, 4, CHUNKS)),
            dma((8, CHUNKS)),
            dma((8, CHUNKS)),
            dma((8, CHUNKS)),
        ],
        compiler_params=pltpu.CompilerParams(
            collective_id=0, has_side_effects=True, vmem_limit_bytes=24 * 2**20
        ),
        name="gather",
    )(
        child_pattern,
        child_sources.T,
        child_classes.T,
        child_counts.reshape(4, 128),
        parent_sources,
        parent_classes,
        parent_counts,
        child_table.transpose(1, 2, 3, 0),
        theta_index.T,
        theta_weight.T,
        phi_index.T,
        phi_weight.T,
        shift_angle.reshape(128, 128),
    )
    child_incoming, pattern, incoming = pl.pallas_call(
        list_kernel,
        out_shape=(
            jax.ShapeDtypeStruct((32, 2, 8, 64), f32),
            jax.ShapeDtypeStruct((128, 128), f32),
            jax.ShapeDtypeStruct((128, 128), f32),
        ),
        in_specs=[vmem] * 7,
        out_specs=(hbm, hbm, hbm),
        scratch_shapes=[
            pltpu.SMEM((2 * CHILD_ROWS, 128), i32),
            pltpu.SMEM((2 * PARENT_ROWS, 128), i32),
            pltpu.VMEM((32, 2, 8, 64), f32),
            pltpu.VMEM((128, 128), f32),
            dma((5,)),
        ],
        compiler_params=pltpu.CompilerParams(vmem_limit_bytes=24 * 2**20),
        name="lists",
    )(g, f, acc, pg, ci, pi, parent_table.reshape(CLASSES * 32, 128))
    shape = (4, 2, 16, 128)
    return child_incoming, pattern.reshape(shape), incoming.reshape(shape)


def solution(mesh):
    return jax.shard_map(
        local,
        mesh=mesh,
        in_specs=(
            P("clus", None, "ang", None),
            P(), P(), P(), P(), P(), P(),
            P(None, None, "ang", None),
            P(None, None, "ang", None),
            P(), P(),
            P("ang", None),
            P("ang", None),
            P(None, "ang", None),
        ),
        out_specs=(
            P("clus", None, "ang", None),
            P("clus", None, "ang", None),
            P("clus", None, "ang", None),
        ),
        check_vma=False,
    )
```

```python
import functools

import jax
import jax.numpy as jnp
from jax import lax
from jax.experimental import pallas as pl
from jax.experimental.pallas import tpu as pltpu
from jax.sharding import PartitionSpec as P

MESH = pl.DeviceIdType.MESH
SLOTS = 189
CLASSES = 316
HEAD = 96
TAIL = 32
CHUNKS = 2
CHILD_STEPS = -(-(SLOTS - HEAD) // TAIL)
PARENT_STEPS = -(-SLOTS // TAIL)
CHILD_ROWS = 32 * CHILD_STEPS
PARENT_ROWS = 8 * PARENT_STEPS


def rows_at(start, size):
    return pl.ds(pl.multiple_of(start, 8), size)


def gather_kernel(
    pat_hbm, cs_hbm, cc_hbm, ccnt_hbm, ps_hbm, pc_hbm, pcnt_hbm, tab_hbm,
    thi_hbm, thw_hbm, phi_hbm, phw_hbm, ang_hbm,
    g_ref, f_ref, acc_ref, pg_ref, ci_ref, pi_ref,
    pat, sv, cv, ccnt, psv, pcv, pcnt, tab, thi, thw, phi, phw, ang,
    own, hs, hr, zs, ta, sa_s, sa_c,
    loc, smsem, hsend, hrecv, csend, crecv, cssend, csrecv, psend, precv, pssend, psrecv,
):
    r = lax.axis_index("clus")
    a = lax.axis_index("ang")
    sib = r + 1 - 2 * lax.rem(r, 2)
    up, down = lax.rem(r + 2, 16), lax.rem(r + 14, 16)
    ahead, behind = lax.rem(a + 1, 16), lax.rem(a + 15, 16)

    lane_block = pl.ds(pl.multiple_of(lax.div(r, 4) * 128, 128), 128)
    row_block = rows_at(lax.div(r, 2) * 8, 8)
    locals_ = [
        (pat_hbm, pat),
        (cs_hbm.at[:, lane_block], sv),
        (cc_hbm.at[:, lane_block], cv),
        (ccnt_hbm, ccnt),
        (ps_hbm.at[row_block, :], psv),
        (pc_hbm.at[row_block, :], pcv),
        (pcnt_hbm, pcnt),
        (thi_hbm, thi),
        (thw_hbm, thw),
        (phi_hbm, phi),
        (phw_hbm, phw),
        (ang_hbm, ang),
        (tab_hbm, tab),
    ]
    copies = [pltpu.make_async_copy(src, dst, loc.at[i]) for i, (src, dst) in enumerate(locals_)]
    for copy in copies:
        copy.start()

    barrier = pltpu.get_barrier_semaphore()
    for target in (up, down, sib):
        pl.semaphore_signal(barrier, inc=1, device_id={"clus": target}, device_id_type=MESH)
    for target in (ahead, behind):
        pl.semaphore_signal(barrier, inc=1, device_id={"ang": target}, device_id_type=MESH)
    pl.semaphore_wait(barrier, 5)

    def mover(buffer, block_rows, send, recv, sib_send, sib_recv):
        size = block_rows // CHUNKS

        def part(owner, ch):
            return buffer.at[rows_at(owner * block_rows + ch * size, size), :]

        def ring(way, step, ch):
            back = 16 - 2 * (step - 1) if way == 0 else 2 * (step - 1)
            block = part(lax.rem(r + back, 16), ch)
            k = (8 - step) if way == 0 else step
            return pltpu.make_async_remote_copy(
                src_ref=block, dst_ref=block,
                send_sem=send.at[way, step - 1, ch], recv_sem=recv.at[k, ch],
                device_id={"clus": up if way == 0 else down}, device_id_type=MESH,
            )

        def arrived(way, step, ch):
            k = (8 - step) if way == 0 else step
            block = part(lax.rem(r + 2 * k, 16), ch)
            pltpu.make_async_remote_copy(
                src_ref=block, dst_ref=block,
                send_sem=send.at[way, step - 1, ch], recv_sem=recv.at[k, ch],
                device_id={"clus": up if way == 0 else down}, device_id_type=MESH,
            ).wait_recv()

        def side(k, ch, mine=True):
            block = part(lax.rem((r if mine else sib) + 2 * k, 16), ch)
            return pltpu.make_async_remote_copy(
                src_ref=block, dst_ref=block,
                send_sem=sib_send.at[k, ch], recv_sem=sib_recv.at[k, ch],
                device_id={"clus": sib}, device_id_type=MESH,
            )

        def uses(way, step, ch):
            return step < 4 or (ch < CHUNKS // 2) == (way == 0)

        def first(ch):
            for way in (0, 1):
                ring(way, 1, ch).start()
            side(0, ch).start()

        def onward(step, ch):
            for way in (0, 1):
                if uses(way, step, ch):
                    arrived(way, step, ch)
                    if step < 4 and uses(way, step + 1, ch):
                        ring(way, step + 1, ch).start()
                    side((8 - step) if way == 0 else step, ch).start()

        def landed():
            for k in range(8):
                for ch in range(CHUNKS):
                    side(k, ch, mine=False).wait_recv()

        def drained():
            for ch in range(CHUNKS):
                for step in range(1, 5):
                    for way in (0, 1):
                        if uses(way, step, ch):
                            ring(way, step, ch).wait_send()
                for k in range(8):
                    side(k, ch).wait_send()

        return first, onward, landed, drained

    c_first, c_onward, c_landed, c_drained = mover(g_ref, 256, csend, crecv, cssend, csrecv)
    p_first, p_onward, p_landed, p_drained = mover(pg_ref, 128, psend, precv, pssend, psrecv)

    copies[0].wait()
    size = 32 // CHUNKS
    for ch in range(CHUNKS):
        x = pat[ch * size:(ch + 1) * size]
        x = jnp.concatenate([x[:, 0], x[:, 1]], axis=2).reshape(size * 8, 128)
        own[ch * size * 8:(ch + 1) * size * 8, :] = x
        g_ref[rows_at(r * 256 + ch * size * 8, size * 8), :] = x
        c_first(ch)

    halo = []
    for way in (0, 1):
        for j in range(2):
            hs[way, j * 32:(j + 1) * 32, :] = own[pl.ds((6 if way == 0 else 0) + j, 32, stride=8), :]
        copy = pltpu.make_async_remote_copy(
            src_ref=hs.at[way], dst_ref=hr.at[way], send_sem=hsend.at[way], recv_sem=hrecv.at[way],
            device_id={"ang": ahead if way == 0 else behind}, device_id_type=MESH,
        )
        copy.start()
        halo.append(copy)

    for i in (1, 2, 3):
        copies[i].wait()
    count_row = ccnt[pl.ds(lax.div(r, 4), 1), :]
    own_rows = rows_at(lax.rem(r, 4) * 32, 32)
    slot = lax.broadcasted_iota(jnp.int32, (128, 128), 0)

    def lists(start, stop):
        s, c = sv[start:stop, :], cv[start:stop, :]
        live = slot[:stop - start] + start < count_row
        s = jnp.where(live, s, 0) * 8
        c = jnp.where(live, c, CLASSES) * 16
        return s, c

    s, c = lists(0, 128)
    ta[0] = lax.shift_right_logical(s, 3).T
    ta[1] = lax.shift_right_logical(c, 4).T
    fill = [
        pltpu.make_async_copy(ta.at[0, own_rows, :], sa_s, smsem.at[0]),
        pltpu.make_async_copy(ta.at[1, own_rows, :], sa_c, smsem.at[1]),
    ]
    for copy in fill:
        copy.start()

    c_onward(1, 0)

    s, c = lists(HEAD, SLOTS)
    rest = 128 - (SLOTS - HEAD)
    s = jnp.concatenate([s, jnp.zeros((rest, 128), jnp.int32)], axis=0)
    c = jnp.concatenate([c, jnp.full((rest, 128), CLASSES * 16, jnp.int32)], axis=0)
    c = jnp.where(slot == 127, count_row, c)
    ta[2] = s.T
    ta[3] = c.T
    ts, tc = ta[2, own_rows, :], ta[3, own_rows, :]
    for i in range(CHILD_STEPS):
        ci_ref[i * 32:(i + 1) * 32, :] = pltpu.roll(ts, (128 - i * TAIL) % 128, 1) if i else ts
        ci_ref[CHILD_ROWS + i * 32:CHILD_ROWS + (i + 1) * 32, :] = (
            pltpu.roll(tc, (128 - i * TAIL) % 128, 1) if i else tc
        )

    for i in (4, 5, 6):
        copies[i].wait()
    line = lax.broadcasted_iota(jnp.int32, (8, 128), 0)
    lane = lax.broadcasted_iota(jnp.int32, (8, 128), 1)
    counts = jnp.zeros((8, 128), jnp.int32)
    for i in range(8):
        counts = jnp.where(line == i, pcnt[lax.div(r, 2) * 8 + i], counts)
    pads = jnp.zeros((8, 256 - SLOTS), jnp.int32)
    for half in range(2):
        if half == 0:
            s, c = psv[:, :128], pcv[:, :128]
        else:
            s = jnp.concatenate([psv[:, 128:], pads], axis=1)
            c = jnp.concatenate([pcv[:, 128:], pads], axis=1)
        live = lane + half * 128 < counts
        s = jnp.where(live, s, 64) * 32
        c = jnp.where(live, c, 0) * 32
        for i in range(half * 128 // TAIL, min((half + 1) * 128 // TAIL, PARENT_STEPS)):
            turn = (128 - (i * TAIL - half * 128)) % 128
            si = pltpu.roll(s, turn, 1) if turn else s
            cj = pltpu.roll(c, turn, 1) if turn else c
            pi_ref[i * 8:(i + 1) * 8, :] = si
            pi_ref[PARENT_ROWS + i * 8:PARENT_ROWS + (i + 1) * 8, :] = jnp.where(lane == 127, counts, cj)
    pg_ref[2048:2080, :] = jnp.zeros((32, 128), jnp.float32)

    c_onward(1, 1)

    copies[12].wait()

    def operators(col):
        for b in range(3):
            lo, hi = b * 128, min((b + 1) * 128, CLASSES)
            x = jnp.concatenate([tab[0, col, :, lo:hi], tab[1, col, :, lo:hi]], axis=0)
            if hi - lo < 128:
                x = jnp.concatenate([x, jnp.zeros((128, 128 - (hi - lo)), jnp.float32)], axis=1)
            y = x.T
            f_ref[pl.ds(lo * 16 + col, 128, stride=16), :] = y
            f_ref[pl.ds(lo * 16 + col + 8, 128, stride=16), :] = pltpu.roll(y, 64, 1)

    for col in range(4):
        operators(col)
    c_onward(2, 0)
    for col in range(4, 8):
        operators(col)
    c_onward(2, 1)

    for i in (7, 8, 9, 10, 11):
        copies[i].wait()
    for copy in halo:
        copy.wait_recv()
    offset = lax.rem(phi[...] - a * 8 + (2 + 128), 128)
    weights = phw[...]
    base = lax.shift_right_logical(lax.broadcasted_iota(jnp.int32, (1, 16), 1), 1)
    taps = []
    for d in range(5):
        tap = jnp.zeros((1, 16), jnp.float32)
        for i in range(4):
            tap = tap + jnp.where(offset[i:i + 1, :] == base + d, weights[i:i + 1, :], 0.0)
        taps.append(tap)
    cols = [hr[0, :32, :], hr[0, 32:, :]]
    cols += [own[pl.ds(j, 32, stride=8), :] for j in range(8)]
    cols += [hr[1, :32, :], hr[1, 32:, :]]
    for j in range(16):
        z = jnp.zeros((32, 128), jnp.float32)
        for d in range(5):
            z = z + taps[d][:, j:j + 1] * cols[j // 2 + d]
        zs[pl.ds(j, 32, stride=16), :] = z

    c_onward(3, 0)

    row = lax.broadcasted_iota(jnp.int32, (64, 128), 0)
    theta = jnp.zeros((64, 128), jnp.float32)
    for i in range(4):
        theta = theta + jnp.where(thi[i:i + 1, :] == row, thw[i:i + 1, :], 0.0)
    blank = jnp.zeros((64, 128), jnp.float32)
    pair = jnp.concatenate(
        [jnp.concatenate([theta, blank], axis=1), jnp.concatenate([blank, theta], axis=1)], axis=0
    )
    angles = ang[...]
    cosine, sine = jnp.cos(angles), jnp.sin(angles)

    c_onward(3, 1)

    for parent in range(4):
        y = jnp.dot(
            zs[parent * 128:(parent + 1) * 128, :], pair,
            precision=lax.Precision.HIGHEST, preferred_element_type=jnp.float32,
        )
        re = y[:, :128] * cosine - y[:, 128:] * sine
        im = y[:, :128] * sine + y[:, 128:] * cosine
        re = jnp.sum(re.reshape(8, 16, 128), axis=0)
        im = jnp.sum(im.reshape(8, 16, 128), axis=0)
        pg_ref[rows_at(r * 128 + parent * 32, 16), :] = re
        pg_ref[rows_at(r * 128 + parent * 32 + 16, 16), :] = im
        if parent % 2:
            p_first(parent // 2)

    for ch in range(CHUNKS):
        c_onward(4, ch)
    for copy in fill:
        copy.wait()
    c_landed()

    events = {}
    for i, (step, ch) in enumerate([(s, h) for s in range(1, 5) for h in range(CHUNKS)]):
        events.setdefault(min(2 + 4 * i, 31), []).append(functools.partial(p_onward, step, ch))

    g3, f4 = g_ref.reshape(512, 8, 128), f_ref.reshape(384, 2, 8, 128)

    def head(p, carry):
        zero = jnp.zeros((8, 128), jnp.float32)
        one, two = zero, zero
        for m in range(HEAD):
            s, c = sa_s[p, m], sa_c[p, m]
            x = g3[s]
            one = one + x * f4[c, 0]
            two = two + x * f4[c, 1]
        acc_ref[rows_at(p * 16, 8), :] = one
        acc_ref[rows_at(p * 16 + 8, 8), :] = two
        for at, todo in events.items():
            @pl.when(p == at)
            def _():
                for go in todo:
                    go()
        return carry

    lax.fori_loop(0, 32, head, 0)

    p_landed()
    for copy in halo:
        copy.wait_send()
    c_drained()
    p_drained()


def list_kernel(
    g_ref, f_ref, acc_ref, pg_ref, ci_ref, pi_ref, pt_ref,
    child_out, pattern_out, incoming_out,
    ci, pi, child, incoming, sem,
):
    r = lax.axis_index("clus")
    fill_p = pltpu.make_async_copy(pi_ref, pi, sem.at[0])
    fill_c = pltpu.make_async_copy(ci_ref, ci, sem.at[1])
    fill_p.start()
    fill_c.start()
    pattern = pltpu.make_async_copy(pg_ref.at[rows_at(r * 128, 128), :], pattern_out, sem.at[2])
    pattern.start()
    fill_p.wait()

    def parent(p, carry):
        line = lax.rem(r, 2) * 4 + p
        steps = lax.div(pi[PARENT_ROWS + line, 127] + (TAIL - 1), TAIL)

        def step(i, total):
            re, im = total
            for m in range(TAIL):
                s = pl.multiple_of(pi[i * 8 + line, m], 32)
                c = pl.multiple_of(pi[PARENT_ROWS + i * 8 + line, m], 32)
                sr, si = pg_ref[pl.ds(s, 16), :], pg_ref[pl.ds(s + 16, 16), :]
                tr, ti = pt_ref[pl.ds(c, 16), :], pt_ref[pl.ds(c + 16, 16), :]
                re = re + (sr * tr - si * ti)
                im = im + (sr * ti + si * tr)
            return re, im

        zero = jnp.zeros((16, 128), jnp.float32)
        re, im = lax.fori_loop(0, steps, step, (zero, zero))
        incoming[rows_at(p * 32, 16), :] = re
        incoming[rows_at(p * 32 + 16, 16), :] = im
        return carry

    lax.fori_loop(0, 4, parent, 0)
    done = pltpu.make_async_copy(incoming, incoming_out, sem.at[3])
    done.start()
    fill_c.wait()

    def tail(p, carry):
        more = jnp.maximum(ci[CHILD_ROWS + p, 127] - HEAD, 0)
        steps = lax.div(more + (TAIL - 1), TAIL)

        def step(i, total):
            one, two = total
            for m in range(TAIL):
                s = pl.multiple_of(ci[i * 32 + p, m], 8)
                c = pl.multiple_of(ci[CHILD_ROWS + i * 32 + p, m], 16)
                x = g_ref[pl.ds(s, 8), :]
                one = one + x * f_ref[pl.ds(c, 8), :]
                two = two + x * f_ref[pl.ds(c + 8, 8), :]
            return one, two

        start = (acc_ref[rows_at(p * 16, 8), :], acc_ref[rows_at(p * 16 + 8, 8), :])
        one, two = lax.fori_loop(0, steps, step, start)
        child[p, 0] = (one - pltpu.roll(one, 64, 1))[:, :64]
        child[p, 1] = (two + pltpu.roll(two, 64, 1))[:, :64]
        return carry

    lax.fori_loop(0, 32, tail, 0)
    last = pltpu.make_async_copy(child, child_out, sem.at[4])
    last.start()
    pattern.wait()
    done.wait()
    last.wait()


def local(
    child_pattern, child_sources, child_classes, child_counts,
    parent_sources, parent_classes, parent_counts,
    child_table, parent_table, theta_index, theta_weight, phi_index, phi_weight, shift_angle,
):
    f32, i32 = jnp.float32, jnp.int32
    hbm = pl.BlockSpec(memory_space=pltpu.HBM)
    vmem = pl.BlockSpec(memory_space=pltpu.VMEM)
    dma = pltpu.SemaphoreType.DMA
    g, f, acc, pg, ci, pi = pl.pallas_call(
        gather_kernel,
        out_shape=(
            jax.ShapeDtypeStruct((4096, 128), f32),
            jax.ShapeDtypeStruct((6144, 128), f32),
            jax.ShapeDtypeStruct((512, 128), f32),
            jax.ShapeDtypeStruct((2080, 128), f32),
            jax.ShapeDtypeStruct((2 * CHILD_ROWS, 128), i32),
            jax.ShapeDtypeStruct((2 * PARENT_ROWS, 128), i32),
        ),
        in_specs=[hbm] * 13,
        out_specs=(vmem,) * 6,
        scratch_shapes=[
            pltpu.VMEM((32, 2, 8, 64), f32),
            pltpu.VMEM((SLOTS, 128), i32),
            pltpu.VMEM((SLOTS, 128), i32),
            pltpu.VMEM((4, 128), i32),
            pltpu.VMEM((8, SLOTS), i32),
            pltpu.VMEM((8, SLOTS), i32),
            pltpu.SMEM((64,), i32),
            pltpu.VMEM((2, 8, 64, CLASSES), f32),
            pltpu.VMEM((4, 128), i32),
            pltpu.VMEM((4, 128), f32),
            pltpu.VMEM((4, 16), i32),
            pltpu.VMEM((4, 16), f32),
            pltpu.VMEM((128, 128), f32),
            pltpu.VMEM((256, 128), f32),
            pltpu.VMEM((2, 64, 128), f32),
            pltpu.VMEM((2, 64, 128), f32),
            pltpu.VMEM((512, 128), f32),
            pltpu.VMEM((4, 128, 128), i32),
            pltpu.SMEM((32, 128), i32),
            pltpu.SMEM((32, 128), i32),
            dma((13,)),
            dma((2,)),
            dma((2,)),
            dma((2,)),
            dma((2, 4, CHUNKS)),
            dma((8, CHUNKS)),
            dma((8, CHUNKS)),
            dma((8, CHUNKS)),
            dma((2, 4, CHUNKS)),
            dma((8, CHUNKS)),
            dma((8, CHUNKS)),
            dma((8, CHUNKS)),
        ],
        compiler_params=pltpu.CompilerParams(
            collective_id=0, has_side_effects=True, vmem_limit_bytes=24 * 2**20
        ),
        cost_estimate=pl.CostEstimate(flops=30_000_000_000, bytes_accessed=8_000_000, transcendentals=0),
        name="gather",
    )(*(pltpu.with_memory_space_constraint(x, pltpu.HBM) for x in (
        child_pattern,
        child_sources.T,
        child_classes.T,
        child_counts.reshape(4, 128),
        parent_sources,
        parent_classes,
        parent_counts,
        child_table.transpose(1, 2, 3, 0),
        theta_index.T,
        theta_weight.T,
        phi_index.T,
        phi_weight.T,
        shift_angle.reshape(128, 128),
    )))
    child_incoming, pattern, incoming = pl.pallas_call(
        list_kernel,
        out_shape=(
            jax.ShapeDtypeStruct((32, 2, 8, 64), f32),
            jax.ShapeDtypeStruct((128, 128), f32),
            jax.ShapeDtypeStruct((128, 128), f32),
        ),
        in_specs=[vmem] * 7,
        out_specs=(hbm, hbm, hbm),
        scratch_shapes=[
            pltpu.SMEM((2 * CHILD_ROWS, 128), i32),
            pltpu.SMEM((2 * PARENT_ROWS, 128), i32),
            pltpu.VMEM((32, 2, 8, 64), f32),
            pltpu.VMEM((128, 128), f32),
            dma((5,)),
        ],
        compiler_params=pltpu.CompilerParams(vmem_limit_bytes=24 * 2**20),
        name="lists",
    )(g, f, acc, pg, ci, pi, parent_table.reshape(CLASSES * 32, 128))
    shape = (4, 2, 16, 128)
    return child_incoming, pattern.reshape(shape), incoming.reshape(shape)


def solution(mesh):
    return jax.shard_map(
        local,
        mesh=mesh,
        in_specs=(
            P("clus", None, "ang", None),
            P(), P(), P(), P(), P(), P(),
            P(None, None, "ang", None),
            P(None, None, "ang", None),
            P(), P(),
            P("ang", None),
            P("ang", None),
            P(None, "ang", None),
        ),
        out_specs=(
            P("clus", None, "ang", None),
            P("clus", None, "ang", None),
            P("clus", None, "ang", None),
        ),
        check_vma=False,
    )
```

```python
import functools

import jax
import jax.numpy as jnp
from jax import lax
from jax.experimental import pallas as pl
from jax.experimental.pallas import tpu as pltpu
from jax.sharding import PartitionSpec as P

MESH = pl.DeviceIdType.MESH
SLOTS = 189
CLASSES = 316
HEAD = 64
CHILD_TAIL = 25
PARENT_TAIL = 27
CHUNKS = 2


def rows_at(start, size):
    return pl.ds(pl.multiple_of(start, 8), size)


def gather_kernel(
    pat_hbm, cs_hbm, cc_hbm, ccnt_hbm, ps_hbm, pc_hbm, pcnt_hbm, tab_hbm,
    thi_hbm, thw_hbm, phi_hbm, phw_hbm, ang_hbm,
    g_ref, f_ref, acc_ref, pg_ref, ci_ref, pi_ref,
    pat, sv, cv, ccnt, psv, pcv, pcnt, tab, thi, thw, phi, phw, ang,
    own, hs, hr, zs, pair, turns, ta, sa_s, sa_c,
    loc, smsem, hsend, hrecv, csend, crecv, cssend, csrecv, psend, precv, pssend, psrecv,
):
    r = lax.axis_index("clus")
    a = lax.axis_index("ang")
    sib = r + 1 - 2 * lax.rem(r, 2)
    up, down = lax.rem(r + 2, 16), lax.rem(r + 14, 16)
    ahead, behind = lax.rem(a + 1, 16), lax.rem(a + 15, 16)

    lane_block = pl.ds(pl.multiple_of(lax.div(r, 4) * 128, 128), 128)
    row_block = rows_at(lax.div(r, 2) * 8, 8)
    locals_ = [
        (pat_hbm, pat),
        (cs_hbm.at[:, lane_block], sv),
        (cc_hbm.at[:, lane_block], cv),
        (ccnt_hbm, ccnt),
        (ps_hbm.at[row_block, :], psv),
        (pc_hbm.at[row_block, :], pcv),
        (pcnt_hbm, pcnt),
        (thi_hbm, thi),
        (thw_hbm, thw),
        (phi_hbm, phi),
        (phw_hbm, phw),
        (ang_hbm, ang),
        (tab_hbm, tab),
    ]
    copies = [pltpu.make_async_copy(src, dst, loc.at[i]) for i, (src, dst) in enumerate(locals_)]
    for copy in copies:
        copy.start()

    barrier = pltpu.get_barrier_semaphore()
    for target in (up, down, sib):
        pl.semaphore_signal(barrier, inc=1, device_id={"clus": target}, device_id_type=MESH)
    for target in (ahead, behind):
        pl.semaphore_signal(barrier, inc=1, device_id={"ang": target}, device_id_type=MESH)
    pl.semaphore_wait(barrier, 5)

    def mover(buffer, block_rows, send, recv, sib_send, sib_recv):
        size = block_rows // CHUNKS

        def part(owner, ch):
            return buffer.at[rows_at(owner * block_rows + ch * size, size), :]

        def ring(way, step, ch):
            back = 16 - 2 * (step - 1) if way == 0 else 2 * (step - 1)
            block = part(lax.rem(r + back, 16), ch)
            k = (8 - step) if way == 0 else step
            return pltpu.make_async_remote_copy(
                src_ref=block, dst_ref=block,
                send_sem=send.at[way, step - 1, ch], recv_sem=recv.at[k, ch],
                device_id={"clus": up if way == 0 else down}, device_id_type=MESH,
            )

        def arrived(way, step, ch):
            k = (8 - step) if way == 0 else step
            block = part(lax.rem(r + 2 * k, 16), ch)
            pltpu.make_async_remote_copy(
                src_ref=block, dst_ref=block,
                send_sem=send.at[way, step - 1, ch], recv_sem=recv.at[k, ch],
                device_id={"clus": up if way == 0 else down}, device_id_type=MESH,
            ).wait_recv()

        def side(k, ch, mine=True):
            block = part(lax.rem((r if mine else sib) + 2 * k, 16), ch)
            return pltpu.make_async_remote_copy(
                src_ref=block, dst_ref=block,
                send_sem=sib_send.at[k, ch], recv_sem=sib_recv.at[k, ch],
                device_id={"clus": sib}, device_id_type=MESH,
            )

        def uses(way, step, ch):
            return step < 4 or (ch < CHUNKS // 2) == (way == 0)

        def first(ch):
            for way in (0, 1):
                ring(way, 1, ch).start()
            side(0, ch).start()

        def onward(step, ch):
            for way in (0, 1):
                if uses(way, step, ch):
                    arrived(way, step, ch)
                    if step < 4 and uses(way, step + 1, ch):
                        ring(way, step + 1, ch).start()
                    side((8 - step) if way == 0 else step, ch).start()

        def landed():
            for k in range(8):
                for ch in range(CHUNKS):
                    side(k, ch, mine=False).wait_recv()

        def drained():
            for ch in range(CHUNKS):
                for step in range(1, 5):
                    for way in (0, 1):
                        if uses(way, step, ch):
                            ring(way, step, ch).wait_send()
                for k in range(8):
                    side(k, ch).wait_send()

        return first, onward, landed, drained

    c_first, c_onward, c_landed, c_drained = mover(g_ref, 256, csend, crecv, cssend, csrecv)
    p_first, p_onward, p_landed, p_drained = mover(pg_ref, 128, psend, precv, pssend, psrecv)

    copies[0].wait()
    size = 32 // CHUNKS
    for ch in range(CHUNKS):
        x = pat[ch * size:(ch + 1) * size]
        x = jnp.concatenate([x[:, 0], x[:, 1]], axis=2).reshape(size * 8, 128)
        own[ch * size * 8:(ch + 1) * size * 8, :] = x
        g_ref[rows_at(r * 256 + ch * size * 8, size * 8), :] = x
        c_first(ch)

    halo = []
    for way in (0, 1):
        for j in range(2):
            hs[way, j * 32:(j + 1) * 32, :] = own[pl.ds((6 if way == 0 else 0) + j, 32, stride=8), :]
        copy = pltpu.make_async_remote_copy(
            src_ref=hs.at[way], dst_ref=hr.at[way], send_sem=hsend.at[way], recv_sem=hrecv.at[way],
            device_id={"ang": ahead if way == 0 else behind}, device_id_type=MESH,
        )
        copy.start()
        halo.append(copy)

    for i in (7, 8, 9, 10, 11):
        copies[i].wait()
    row = lax.broadcasted_iota(jnp.int32, (64, 128), 0)
    theta = jnp.zeros((64, 128), jnp.float32)
    for i in range(4):
        theta = theta + jnp.where(thi[i:i + 1, :] == row, thw[i:i + 1, :], 0.0)
    blank = jnp.zeros((64, 128), jnp.float32)
    pair[...] = jnp.concatenate(
        [jnp.concatenate([theta, blank], axis=1), jnp.concatenate([blank, theta], axis=1)], axis=0
    )
    angles = ang[...]
    turns[0] = jnp.cos(angles)
    turns[1] = jnp.sin(angles)
    offset = lax.rem(phi[...] - a * 8 + (2 + 128), 128)
    weights = phw[...]
    base = lax.shift_right_logical(lax.broadcasted_iota(jnp.int32, (1, 16), 1), 1)
    taps = []
    for d in range(5):
        tap = jnp.zeros((1, 16), jnp.float32)
        for i in range(4):
            tap = tap + jnp.where(offset[i:i + 1, :] == base + d, weights[i:i + 1, :], 0.0)
        taps.append(tap)

    for copy in halo:
        copy.wait_recv()
    cols = [hr[0, :32, :], hr[0, 32:, :]]
    cols += [own[pl.ds(j, 32, stride=8), :] for j in range(8)]
    cols += [hr[1, :32, :], hr[1, 32:, :]]
    for j in range(16):
        z = jnp.zeros((32, 128), jnp.float32)
        for d in range(5):
            z = z + taps[d][:, j:j + 1] * cols[j // 2 + d]
        zs[pl.ds(j, 32, stride=16), :] = z

    for parent in range(4):
        y = jnp.dot(
            zs[parent * 128:(parent + 1) * 128, :], pair[...],
            precision=lax.Precision.HIGHEST, preferred_element_type=jnp.float32,
        )
        re = y[:, :128] * turns[0] - y[:, 128:] * turns[1]
        im = y[:, :128] * turns[1] + y[:, 128:] * turns[0]
        re = jnp.sum(re.reshape(8, 16, 128), axis=0)
        im = jnp.sum(im.reshape(8, 16, 128), axis=0)
        pg_ref[rows_at(r * 128 + parent * 32, 16), :] = re
        pg_ref[rows_at(r * 128 + parent * 32 + 16, 16), :] = im
        if parent == 1:
            c_onward(1, 0)
            c_onward(1, 1)
            p_first(0)
    p_first(1)
    pg_ref[2048:2080, :] = jnp.zeros((32, 128), jnp.float32)

    for i in (1, 2, 3):
        copies[i].wait()
    count_row = ccnt[pl.ds(lax.div(r, 4), 1), :]
    own_rows = rows_at(lax.rem(r, 4) * 32, 32)
    slot = lax.broadcasted_iota(jnp.int32, (128, 128), 0)

    def lists(start, stop):
        s, c = sv[start:stop, :], cv[start:stop, :]
        live = slot[:stop - start] + start < count_row
        return jnp.where(live, s, 0), jnp.where(live, c, CLASSES)

    s, c = lists(0, 128)
    ta[0] = s.T
    ta[1] = c.T
    fill = [
        pltpu.make_async_copy(ta.at[0, own_rows, :], sa_s, smsem.at[0]),
        pltpu.make_async_copy(ta.at[1, own_rows, :], sa_c, smsem.at[1]),
    ]
    for copy in fill:
        copy.start()

    s, c = lists(HEAD, SLOTS)
    rest = 128 - (SLOTS - HEAD)
    s = jnp.concatenate([s * 8, jnp.zeros((rest, 128), jnp.int32)], axis=0)
    c = jnp.concatenate([c * 16, jnp.full((rest, 128), CLASSES * 16, jnp.int32)], axis=0)
    c = jnp.where(slot == 127, count_row, c)
    ta[2] = s.T
    ta[3] = c.T
    ci_ref[:32, :] = ta[2, own_rows, :]
    ci_ref[32:, :] = ta[3, own_rows, :]

    c_onward(2, 0)
    c_onward(2, 1)

    for i in (4, 5, 6):
        copies[i].wait()
    line = lax.broadcasted_iota(jnp.int32, (8, 128), 0)
    lane = lax.broadcasted_iota(jnp.int32, (8, 128), 1)
    counts = jnp.zeros((8, 128), jnp.int32)
    for i in range(8):
        counts = jnp.where(line == i, pcnt[lax.div(r, 2) * 8 + i], counts)
    pads = jnp.zeros((8, 256 - SLOTS), jnp.int32)
    for half in range(2):
        if half == 0:
            s, c = psv[:, :128], pcv[:, :128]
        else:
            s = jnp.concatenate([psv[:, 128:], pads], axis=1)
            c = jnp.concatenate([pcv[:, 128:], pads], axis=1)
        live = lane + half * 128 < counts
        s = jnp.where(live, s, 64) * 32
        c = jnp.where(live, c, 0) * 32
        pi_ref[half * 8:half * 8 + 8, :] = s
        pi_ref[16 + half * 8:16 + half * 8 + 8, :] = jnp.where(lane == 127, counts, c) if half else c

    p_onward(1, 0)
    p_onward(1, 1)

    copies[12].wait()

    def operators(col):
        for b in range(3):
            lo, hi = b * 128, min((b + 1) * 128, CLASSES)
            x = jnp.concatenate([tab[0, col, :, lo:hi], tab[1, col, :, lo:hi]], axis=0)
            if hi - lo < 128:
                x = jnp.concatenate([x, jnp.zeros((128, 128 - (hi - lo)), jnp.float32)], axis=1)
            y = x.T
            f_ref[pl.ds(lo * 16 + col, 128, stride=16), :] = y
            f_ref[pl.ds(lo * 16 + col + 8, 128, stride=16), :] = pltpu.roll(y, 64, 1)

    for col in range(4):
        operators(col)
    c_onward(3, 0)
    c_onward(3, 1)
    for col in range(4, 8):
        operators(col)
    p_onward(2, 0)
    p_onward(2, 1)

    for ch in range(CHUNKS):
        c_onward(4, ch)
    for copy in fill:
        copy.wait()
    c_landed()
    p_onward(3, 0)
    p_onward(3, 1)

    events = {16: [functools.partial(p_onward, 4, ch) for ch in range(CHUNKS)]}

    g3, f4 = g_ref.reshape(512, 8, 128), f_ref.reshape(384, 2, 8, 128)

    def head(p, carry):
        zero = jnp.zeros((8, 128), jnp.float32)
        one, two = zero, zero
        for m in range(HEAD):
            s, c = sa_s[p, m], sa_c[p, m]
            x = g3[s]
            one = one + x * f4[c, 0]
            two = two + x * f4[c, 1]
        acc_ref[rows_at(p * 16, 8), :] = one
        acc_ref[rows_at(p * 16 + 8, 8), :] = two
        for at, todo in events.items():
            @pl.when(p == at)
            def _():
                for go in todo:
                    go()
        return carry

    lax.fori_loop(0, 32, head, 0)

    p_landed()
    for copy in halo:
        copy.wait_send()
    c_drained()
    p_drained()


def list_kernel(
    g_ref, f_ref, acc_ref, pg_ref, ci_ref, pi_ref, pt_ref,
    child_out, pattern_out, incoming_out,
    ci, pi, child, incoming, sem,
):
    r = lax.axis_index("clus")
    fill_p = pltpu.make_async_copy(pi_ref, pi, sem.at[0])
    fill_c = pltpu.make_async_copy(ci_ref, ci, sem.at[1])
    fill_p.start()
    fill_c.start()
    pattern = pltpu.make_async_copy(pg_ref.at[rows_at(r * 128, 128), :], pattern_out, sem.at[2])
    pattern.start()
    fill_p.wait()

    def run(count, width, last, chunk, total, start=0):
        if start >= last:
            return total
        stop = min(start + width, last)

        def more(total):
            return run(count, width, last, chunk, chunk(start, stop, total), stop)

        return lax.cond(count > start, more, lambda total: total, total)

    def parent(p, carry):
        line = lax.rem(r, 2) * 4 + p

        def chunk(start, stop, total):
            re, im = total
            for m in range(start, stop):
                row = line + 8 * (m // 128)
                s = pl.multiple_of(pi[row, m % 128], 32)
                c = pl.multiple_of(pi[16 + row, m % 128], 32)
                sr, si = pg_ref[pl.ds(s, 16), :], pg_ref[pl.ds(s + 16, 16), :]
                tr, ti = pt_ref[pl.ds(c, 16), :], pt_ref[pl.ds(c + 16, 16), :]
                re = re + (sr * tr - si * ti)
                im = im + (sr * ti + si * tr)
            return re, im

        zero = jnp.zeros((16, 128), jnp.float32)
        re, im = run(pi[24 + line, 127], PARENT_TAIL, SLOTS, chunk, (zero, zero))
        incoming[rows_at(p * 32, 16), :] = re
        incoming[rows_at(p * 32 + 16, 16), :] = im
        return carry

    lax.fori_loop(0, 4, parent, 0)
    done = pltpu.make_async_copy(incoming, incoming_out, sem.at[3])
    done.start()
    fill_c.wait()

    def tail(p, carry):
        def chunk(start, stop, total):
            one, two = total
            for m in range(start, stop):
                s = pl.multiple_of(ci[p, m], 8)
                c = pl.multiple_of(ci[32 + p, m], 16)
                x = g_ref[pl.ds(s, 8), :]
                one = one + x * f_ref[pl.ds(c, 8), :]
                two = two + x * f_ref[pl.ds(c + 8, 8), :]
            return one, two

        start = (acc_ref[rows_at(p * 16, 8), :], acc_ref[rows_at(p * 16 + 8, 8), :])
        one, two = run(ci[32 + p, 127] - HEAD, CHILD_TAIL, SLOTS - HEAD, chunk, start)
        child[p, 0] = (one - pltpu.roll(one, 64, 1))[:, :64]
        child[p, 1] = (two + pltpu.roll(two, 64, 1))[:, :64]
        return carry

    lax.fori_loop(0, 32, tail, 0)
    last = pltpu.make_async_copy(child, child_out, sem.at[4])
    last.start()
    pattern.wait()
    done.wait()
    last.wait()


def local(
    child_pattern, child_sources, child_classes, child_counts,
    parent_sources, parent_classes, parent_counts,
    child_table, parent_table, theta_index, theta_weight, phi_index, phi_weight, shift_angle,
):
    f32, i32 = jnp.float32, jnp.int32
    hbm = pl.BlockSpec(memory_space=pltpu.HBM)
    vmem = pl.BlockSpec(memory_space=pltpu.VMEM)
    dma = pltpu.SemaphoreType.DMA
    g, f, acc, pg, ci, pi = pl.pallas_call(
        gather_kernel,
        out_shape=(
            jax.ShapeDtypeStruct((4096, 128), f32),
            jax.ShapeDtypeStruct((6144, 128), f32),
            jax.ShapeDtypeStruct((512, 128), f32),
            jax.ShapeDtypeStruct((2080, 128), f32),
            jax.ShapeDtypeStruct((64, 128), i32),
            jax.ShapeDtypeStruct((32, 128), i32),
        ),
        in_specs=[hbm] * 13,
        out_specs=(vmem,) * 6,
        scratch_shapes=[
            pltpu.VMEM((32, 2, 8, 64), f32),
            pltpu.VMEM((SLOTS, 128), i32),
            pltpu.VMEM((SLOTS, 128), i32),
            pltpu.VMEM((4, 128), i32),
            pltpu.VMEM((8, SLOTS), i32),
            pltpu.VMEM((8, SLOTS), i32),
            pltpu.SMEM((64,), i32),
            pltpu.VMEM((2, 8, 64, CLASSES), f32),
            pltpu.VMEM((4, 128), i32),
            pltpu.VMEM((4, 128), f32),
            pltpu.VMEM((4, 16), i32),
            pltpu.VMEM((4, 16), f32),
            pltpu.VMEM((128, 128), f32),
            pltpu.VMEM((256, 128), f32),
            pltpu.VMEM((2, 64, 128), f32),
            pltpu.VMEM((2, 64, 128), f32),
            pltpu.VMEM((512, 128), f32),
            pltpu.VMEM((128, 256), f32),
            pltpu.VMEM((2, 128, 128), f32),
            pltpu.VMEM((4, 128, 128), i32),
            pltpu.SMEM((32, 128), i32),
            pltpu.SMEM((32, 128), i32),
            dma((13,)),
            dma((2,)),
            dma((2,)),
            dma((2,)),
            dma((2, 4, CHUNKS)),
            dma((8, CHUNKS)),
            dma((8, CHUNKS)),
            dma((8, CHUNKS)),
            dma((2, 4, CHUNKS)),
            dma((8, CHUNKS)),
            dma((8, CHUNKS)),
            dma((8, CHUNKS)),
        ],
        compiler_params=pltpu.CompilerParams(
            collective_id=0, has_side_effects=True, vmem_limit_bytes=24 * 2**20
        ),
        cost_estimate=pl.CostEstimate(flops=30_000_000_000, bytes_accessed=8_000_000, transcendentals=0),
        name="gather",
    )(*(pltpu.with_memory_space_constraint(x, pltpu.HBM) for x in (
        child_pattern,
        child_sources.T,
        child_classes.T,
        child_counts.reshape(4, 128),
        parent_sources,
        parent_classes,
        parent_counts,
        child_table.transpose(1, 2, 3, 0),
        theta_index.T,
        theta_weight.T,
        phi_index.T,
        phi_weight.T,
        shift_angle.reshape(128, 128),
    )))
    child_incoming, pattern, incoming = pl.pallas_call(
        list_kernel,
        out_shape=(
            jax.ShapeDtypeStruct((32, 2, 8, 64), f32),
            jax.ShapeDtypeStruct((128, 128), f32),
            jax.ShapeDtypeStruct((128, 128), f32),
        ),
        in_specs=[vmem] * 7,
        out_specs=(hbm, hbm, hbm),
        scratch_shapes=[
            pltpu.SMEM((64, 128), i32),
            pltpu.SMEM((32, 128), i32),
            pltpu.VMEM((32, 2, 8, 64), f32),
            pltpu.VMEM((128, 128), f32),
            dma((5,)),
        ],
        compiler_params=pltpu.CompilerParams(vmem_limit_bytes=24 * 2**20),
        name="lists",
    )(g, f, acc, pg, ci, pi, parent_table.reshape(CLASSES * 32, 128))
    shape = (4, 2, 16, 128)
    return child_incoming, pattern.reshape(shape), incoming.reshape(shape)


def solution(mesh):
    return jax.shard_map(
        local,
        mesh=mesh,
        in_specs=(
            P("clus", None, "ang", None),
            P(), P(), P(), P(), P(), P(),
            P(None, None, "ang", None),
            P(None, None, "ang", None),
            P(), P(),
            P("ang", None),
            P("ang", None),
            P(None, "ang", None),
        ),
        out_specs=(
            P("clus", None, "ang", None),
            P("clus", None, "ang", None),
            P("clus", None, "ang", None),
        ),
        check_vma=False,
    )
```

```python
import functools

import jax
import jax.numpy as jnp
from jax import lax
from jax.experimental import pallas as pl
from jax.experimental.pallas import tpu as pltpu
from jax.sharding import PartitionSpec as P

MESH = pl.DeviceIdType.MESH
SLOTS = 189
CLASSES = 316
HEAD = 64
CHILD_TAIL = 25
PARENT_TAIL = 27
CHUNKS = 2


def rows_at(start, size):
    return pl.ds(pl.multiple_of(start, 8), size)


def gather_kernel(
    pat_hbm, cs_hbm, cc_hbm, ccnt_hbm, ps_hbm, pc_hbm, pcnt_hbm, tab_hbm,
    thi_hbm, thw_hbm, phi_hbm, phw_hbm, ang_hbm,
    g_ref, f_ref, acc_ref, pg_ref, ci_ref, pi_ref,
    pat, sv, cv, ccnt, psv, pcv, pcnt, tab, thi, thw, phi, phw, ang,
    own, hs, hr, zs, pair, turns, pv, ta, sa_s, sa_c,
    loc, smsem, hsend, hrecv, csend, crecv, cssend, csrecv, psend, precv, pssend, psrecv,
):
    r = lax.axis_index("clus")
    a = lax.axis_index("ang")
    sib = r + 1 - 2 * lax.rem(r, 2)
    up, down = lax.rem(r + 2, 16), lax.rem(r + 14, 16)
    ahead, behind = lax.rem(a + 1, 16), lax.rem(a + 15, 16)

    lane_block = pl.ds(pl.multiple_of(lax.div(r, 4) * 128, 128), 128)
    row_block = rows_at(lax.div(r, 2) * 8, 8)
    locals_ = [
        (pat_hbm, pat),
        (cs_hbm.at[:, lane_block], sv),
        (cc_hbm.at[:, lane_block], cv),
        (ccnt_hbm, ccnt),
        (ps_hbm.at[row_block, :], psv),
        (pc_hbm.at[row_block, :], pcv),
        (pcnt_hbm, pcnt),
        (thi_hbm, thi),
        (thw_hbm, thw),
        (phi_hbm, phi),
        (phw_hbm, phw),
        (ang_hbm, ang),
        (tab_hbm, tab),
    ]
    copies = [pltpu.make_async_copy(src, dst, loc.at[i]) for i, (src, dst) in enumerate(locals_)]
    for copy in copies:
        copy.start()

    barrier = pltpu.get_barrier_semaphore()
    for target in (up, down, sib):
        pl.semaphore_signal(barrier, inc=1, device_id={"clus": target}, device_id_type=MESH)
    for target in (ahead, behind):
        pl.semaphore_signal(barrier, inc=1, device_id={"ang": target}, device_id_type=MESH)
    pl.semaphore_wait(barrier, 5)

    def mover(buffer, block_rows, send, recv, sib_send, sib_recv):
        size = block_rows // CHUNKS

        def part(owner, ch):
            return buffer.at[rows_at(owner * block_rows + ch * size, size), :]

        def ring(way, step, ch):
            back = 16 - 2 * (step - 1) if way == 0 else 2 * (step - 1)
            block = part(lax.rem(r + back, 16), ch)
            k = (8 - step) if way == 0 else step
            return pltpu.make_async_remote_copy(
                src_ref=block, dst_ref=block,
                send_sem=send.at[way, step - 1, ch], recv_sem=recv.at[k, ch],
                device_id={"clus": up if way == 0 else down}, device_id_type=MESH,
            )

        def arrived(way, step, ch):
            k = (8 - step) if way == 0 else step
            block = part(lax.rem(r + 2 * k, 16), ch)
            pltpu.make_async_remote_copy(
                src_ref=block, dst_ref=block,
                send_sem=send.at[way, step - 1, ch], recv_sem=recv.at[k, ch],
                device_id={"clus": up if way == 0 else down}, device_id_type=MESH,
            ).wait_recv()

        def side(k, ch, mine=True):
            block = part(lax.rem((r if mine else sib) + 2 * k, 16), ch)
            return pltpu.make_async_remote_copy(
                src_ref=block, dst_ref=block,
                send_sem=sib_send.at[k, ch], recv_sem=sib_recv.at[k, ch],
                device_id={"clus": sib}, device_id_type=MESH,
            )

        def uses(way, step, ch):
            return step < 4 or (ch < CHUNKS // 2) == (way == 0)

        def first(ch):
            for way in (0, 1):
                ring(way, 1, ch).start()
            side(0, ch).start()

        def onward(step, ch):
            for way in (0, 1):
                if uses(way, step, ch):
                    arrived(way, step, ch)
                    if step < 4 and uses(way, step + 1, ch):
                        ring(way, step + 1, ch).start()
                    side((8 - step) if way == 0 else step, ch).start()

        def landed():
            for k in range(8):
                for ch in range(CHUNKS):
                    side(k, ch, mine=False).wait_recv()

        def drained():
            for ch in range(CHUNKS):
                for step in range(1, 5):
                    for way in (0, 1):
                        if uses(way, step, ch):
                            ring(way, step, ch).wait_send()
                for k in range(8):
                    side(k, ch).wait_send()

        return first, onward, landed, drained

    c_first, c_onward, c_landed, c_drained = mover(g_ref, 256, csend, crecv, cssend, csrecv)
    p_first, p_onward, p_landed, p_drained = mover(pg_ref, 128, psend, precv, pssend, psrecv)

    copies[0].wait()
    size = 32 // CHUNKS
    for ch in range(CHUNKS):
        x = pat[ch * size:(ch + 1) * size]
        x = jnp.concatenate([x[:, 0], x[:, 1]], axis=2).reshape(size * 8, 128)
        own[ch * size * 8:(ch + 1) * size * 8, :] = x
        g_ref[rows_at(r * 256 + ch * size * 8, size * 8), :] = x
        c_first(ch)

    halo = []
    for way in (0, 1):
        for j in range(2):
            hs[way, j * 32:(j + 1) * 32, :] = own[pl.ds((6 if way == 0 else 0) + j, 32, stride=8), :]
        copy = pltpu.make_async_remote_copy(
            src_ref=hs.at[way], dst_ref=hr.at[way], send_sem=hsend.at[way], recv_sem=hrecv.at[way],
            device_id={"ang": ahead if way == 0 else behind}, device_id_type=MESH,
        )
        copy.start()
        halo.append(copy)

    for i in (7, 8, 9, 10, 11):
        copies[i].wait()
    row = lax.broadcasted_iota(jnp.int32, (64, 128), 0)
    theta = jnp.zeros((64, 128), jnp.float32)
    for i in range(4):
        theta = theta + jnp.where(thi[i:i + 1, :] == row, thw[i:i + 1, :], 0.0)
    blank = jnp.zeros((64, 128), jnp.float32)
    pair[...] = jnp.concatenate(
        [jnp.concatenate([theta, blank], axis=1), jnp.concatenate([blank, theta], axis=1)], axis=0
    )
    angles = ang[...]
    turns[0] = jnp.cos(angles)
    turns[1] = jnp.sin(angles)
    offset = lax.rem(phi[...] - a * 8 + (2 + 128), 128)
    weights = phw[...]
    base = lax.shift_right_logical(lax.broadcasted_iota(jnp.int32, (1, 16), 1), 1)
    taps = []
    for d in range(5):
        tap = jnp.zeros((1, 16), jnp.float32)
        for i in range(4):
            tap = tap + jnp.where(offset[i:i + 1, :] == base + d, weights[i:i + 1, :], 0.0)
        taps.append(tap)

    for copy in halo:
        copy.wait_recv()
    cols = [hr[0, :32, :], hr[0, 32:, :]]
    cols += [own[pl.ds(j, 32, stride=8), :] for j in range(8)]
    cols += [hr[1, :32, :], hr[1, 32:, :]]
    for j in range(16):
        z = jnp.zeros((32, 128), jnp.float32)
        for d in range(5):
            z = z + taps[d][:, j:j + 1] * cols[j // 2 + d]
        zs[pl.ds(j, 32, stride=16), :] = z

    for parent in range(4):
        y = jnp.dot(
            zs[parent * 128:(parent + 1) * 128, :], pair[...],
            precision=lax.Precision.HIGHEST, preferred_element_type=jnp.float32,
        )
        re = y[:, :128] * turns[0] - y[:, 128:] * turns[1]
        im = y[:, :128] * turns[1] + y[:, 128:] * turns[0]
        re = jnp.sum(re.reshape(8, 16, 128), axis=0)
        im = jnp.sum(im.reshape(8, 16, 128), axis=0)
        pg_ref[rows_at(r * 128 + parent * 32, 16), :] = re
        pg_ref[rows_at(r * 128 + parent * 32 + 16, 16), :] = im
        if parent == 1:
            c_onward(1, 0)
            c_onward(1, 1)
            p_first(0)
    p_first(1)
    pg_ref[2048:2080, :] = jnp.zeros((32, 128), jnp.float32)

    for i in (1, 2, 3):
        copies[i].wait()
    count_row = ccnt[pl.ds(lax.div(r, 4), 1), :]
    own_rows = rows_at(lax.rem(r, 4) * 32, 32)
    slot = lax.broadcasted_iota(jnp.int32, (128, 128), 0)

    def lists(start, stop):
        s, c = sv[start:stop, :], cv[start:stop, :]
        live = slot[:stop - start] + start < count_row
        return jnp.where(live, s, 0), jnp.where(live, c, CLASSES)

    s, c = lists(0, 128)
    ta[0] = s.T
    ta[1] = c.T
    fill = [
        pltpu.make_async_copy(ta.at[0, own_rows, :], sa_s, smsem.at[0]),
        pltpu.make_async_copy(ta.at[1, own_rows, :], sa_c, smsem.at[1]),
    ]
    for copy in fill:
        copy.start()

    s, c = lists(HEAD, SLOTS)
    rest = 128 - (SLOTS - HEAD)
    s = jnp.concatenate([s * 8, jnp.zeros((rest, 128), jnp.int32)], axis=0)
    c = jnp.concatenate([c * 16, jnp.full((rest, 128), CLASSES * 16, jnp.int32)], axis=0)
    c = jnp.where(slot == 127, count_row, c)
    ta[2] = s.T
    ta[3] = c.T
    fill += [
        pltpu.make_async_copy(ta.at[2, own_rows, :], ci_ref.at[:32, :], smsem.at[2]),
        pltpu.make_async_copy(ta.at[3, own_rows, :], ci_ref.at[32:, :], smsem.at[3]),
    ]
    fill[2].start()
    fill[3].start()

    c_onward(2, 0)
    c_onward(2, 1)

    for i in (4, 5, 6):
        copies[i].wait()
    line = lax.broadcasted_iota(jnp.int32, (8, 128), 0)
    lane = lax.broadcasted_iota(jnp.int32, (8, 128), 1)
    counts = jnp.zeros((8, 128), jnp.int32)
    for i in range(8):
        counts = jnp.where(line == i, pcnt[lax.div(r, 2) * 8 + i], counts)
    pads = jnp.zeros((8, 256 - SLOTS), jnp.int32)
    for half in range(2):
        if half == 0:
            s, c = psv[:, :128], pcv[:, :128]
        else:
            s = jnp.concatenate([psv[:, 128:], pads], axis=1)
            c = jnp.concatenate([pcv[:, 128:], pads], axis=1)
        live = lane + half * 128 < counts
        s = jnp.where(live, s, 64) * 32
        c = jnp.where(live, c, 0) * 32
        pv[half * 8:half * 8 + 8, :] = s
        pv[16 + half * 8:16 + half * 8 + 8, :] = jnp.where(lane == 127, counts, c) if half else c

    fill.append(pltpu.make_async_copy(pv, pi_ref, smsem.at[4]))
    fill[4].start()

    p_onward(1, 0)
    p_onward(1, 1)

    copies[12].wait()

    def operators(col):
        for b in range(3):
            lo, hi = b * 128, min((b + 1) * 128, CLASSES)
            x = jnp.concatenate([tab[0, col, :, lo:hi], tab[1, col, :, lo:hi]], axis=0)
            if hi - lo < 128:
                x = jnp.concatenate([x, jnp.zeros((128, 128 - (hi - lo)), jnp.float32)], axis=1)
            y = x.T
            f_ref[pl.ds(lo * 16 + col, 128, stride=16), :] = y
            f_ref[pl.ds(lo * 16 + col + 8, 128, stride=16), :] = pltpu.roll(y, 64, 1)

    for col in range(4):
        operators(col)
    c_onward(3, 0)
    c_onward(3, 1)
    for col in range(4, 8):
        operators(col)
    p_onward(2, 0)
    p_onward(2, 1)

    for ch in range(CHUNKS):
        c_onward(4, ch)
    p_onward(3, 0)
    p_onward(3, 1)
    for copy in fill:
        copy.wait()
    c_landed()

    events = {16: [functools.partial(p_onward, 4, ch) for ch in range(CHUNKS)]}

    g3, f4 = g_ref.reshape(512, 8, 128), f_ref.reshape(384, 2, 8, 128)

    def head(p, carry):
        zero = jnp.zeros((8, 128), jnp.float32)
        one, two = zero, zero
        for m in range(HEAD):
            s, c = sa_s[p, m], sa_c[p, m]
            x = g3[s]
            one = one + x * f4[c, 0]
            two = two + x * f4[c, 1]
        acc_ref[rows_at(p * 16, 8), :] = one
        acc_ref[rows_at(p * 16 + 8, 8), :] = two
        for at, todo in events.items():
            @pl.when(p == at)
            def _():
                for go in todo:
                    go()
        return carry

    lax.fori_loop(0, 32, head, 0)

    p_landed()
    for copy in halo:
        copy.wait_send()
    c_drained()
    p_drained()


def list_kernel(
    g_ref, f_ref, acc_ref, pg_ref, ci, pi, pt_ref,
    child_out, pattern_out, incoming_out,
    child, incoming, sums, sem,
):
    r = lax.axis_index("clus")
    pattern = pltpu.make_async_copy(pg_ref.at[rows_at(r * 128, 128), :], pattern_out, sem.at[2])
    pattern.start()

    def run(count, width, last, chunk, total, start=0):
        if start >= last:
            return total
        stop = min(start + width, last)

        def more(total):
            return run(count, width, last, chunk, chunk(start, stop, total), stop)

        return lax.cond(count > start, more, lambda total: total, total)

    def parent(p, carry):
        line = lax.rem(r, 2) * 4 + p

        def chunk(start, stop, total):
            re, im = total
            for m in range(start, stop):
                row = line + 8 * (m // 128)
                s = pl.multiple_of(pi[row, m % 128], 32)
                c = pl.multiple_of(pi[16 + row, m % 128], 32)
                sr, si = pg_ref[pl.ds(s, 16), :], pg_ref[pl.ds(s + 16, 16), :]
                tr, ti = pt_ref[pl.ds(c, 16), :], pt_ref[pl.ds(c + 16, 16), :]
                re = re + (sr * tr - si * ti)
                im = im + (sr * ti + si * tr)
            return re, im

        zero = jnp.zeros((16, 128), jnp.float32)
        re, im = run(pi[24 + line, 127], PARENT_TAIL, SLOTS, chunk, (zero, zero))
        incoming[rows_at(p * 32, 16), :] = re
        incoming[rows_at(p * 32 + 16, 16), :] = im
        return carry

    lax.fori_loop(0, 4, parent, 0)
    done = pltpu.make_async_copy(incoming, incoming_out, sem.at[3])
    done.start()

    def tail(p, carry):
        def chunk(start, stop, total):
            one, two = total
            for m in range(start, stop):
                s = pl.multiple_of(ci[p, m], 8)
                c = pl.multiple_of(ci[32 + p, m], 16)
                x = g_ref[pl.ds(s, 8), :]
                one = one + x * f_ref[pl.ds(c, 8), :]
                two = two + x * f_ref[pl.ds(c + 8, 8), :]
            return one, two

        start = (acc_ref[rows_at(p * 16, 8), :], acc_ref[rows_at(p * 16 + 8, 8), :])
        one, two = run(ci[32 + p, 127] - HEAD, CHILD_TAIL, SLOTS - HEAD, chunk, start)
        sums[0, p] = one
        sums[1, p] = two
        return carry

    parts = []
    for i in range(4):
        lax.fori_loop(8 * i, 8 * i + 8, tail, 0)
        group = pl.ds(8 * i, 8)
        one, two = sums[0, group].reshape(64, 128), sums[1, group].reshape(64, 128)
        re, im = one - pltpu.roll(one, 64, 1), two + pltpu.roll(two, 64, 1)
        child[group, 0] = re[:, :64].reshape(8, 8, 64)
        child[group, 1] = im[:, :64].reshape(8, 8, 64)
        parts.append(pltpu.make_async_copy(child.at[group], child_out.at[group], sem.at[4 + i]))
        parts[i].start()
    pattern.wait()
    done.wait()
    for part in parts:
        part.wait()


def local(
    child_pattern, child_sources, child_classes, child_counts,
    parent_sources, parent_classes, parent_counts,
    child_table, parent_table, theta_index, theta_weight, phi_index, phi_weight, shift_angle,
):
    f32, i32 = jnp.float32, jnp.int32
    hbm = pl.BlockSpec(memory_space=pltpu.HBM)
    vmem = pl.BlockSpec(memory_space=pltpu.VMEM)
    dma = pltpu.SemaphoreType.DMA
    g, f, acc, pg, ci, pi = pl.pallas_call(
        gather_kernel,
        out_shape=(
            jax.ShapeDtypeStruct((4096, 128), f32),
            jax.ShapeDtypeStruct((6144, 128), f32),
            jax.ShapeDtypeStruct((512, 128), f32),
            jax.ShapeDtypeStruct((2080, 128), f32),
            pltpu.SMEM((64, 128), i32),
            pltpu.SMEM((32, 128), i32),
        ),
        in_specs=[hbm] * 13,
        out_specs=(vmem,) * 4 + (pl.BlockSpec(memory_space=pltpu.SMEM),) * 2,
        scratch_shapes=[
            pltpu.VMEM((32, 2, 8, 64), f32),
            pltpu.VMEM((SLOTS, 128), i32),
            pltpu.VMEM((SLOTS, 128), i32),
            pltpu.VMEM((4, 128), i32),
            pltpu.VMEM((8, SLOTS), i32),
            pltpu.VMEM((8, SLOTS), i32),
            pltpu.SMEM((64,), i32),
            pltpu.VMEM((2, 8, 64, CLASSES), f32),
            pltpu.VMEM((4, 128), i32),
            pltpu.VMEM((4, 128), f32),
            pltpu.VMEM((4, 16), i32),
            pltpu.VMEM((4, 16), f32),
            pltpu.VMEM((128, 128), f32),
            pltpu.VMEM((256, 128), f32),
            pltpu.VMEM((2, 64, 128), f32),
            pltpu.VMEM((2, 64, 128), f32),
            pltpu.VMEM((512, 128), f32),
            pltpu.VMEM((128, 256), f32),
            pltpu.VMEM((2, 128, 128), f32),
            pltpu.VMEM((32, 128), i32),
            pltpu.VMEM((4, 128, 128), i32),
            pltpu.SMEM((32, 128), i32),
            pltpu.SMEM((32, 128), i32),
            dma((13,)),
            dma((5,)),
            dma((2,)),
            dma((2,)),
            dma((2, 4, CHUNKS)),
            dma((8, CHUNKS)),
            dma((8, CHUNKS)),
            dma((8, CHUNKS)),
            dma((2, 4, CHUNKS)),
            dma((8, CHUNKS)),
            dma((8, CHUNKS)),
            dma((8, CHUNKS)),
        ],
        compiler_params=pltpu.CompilerParams(
            collective_id=0, has_side_effects=True, vmem_limit_bytes=24 * 2**20
        ),
        cost_estimate=pl.CostEstimate(flops=30_000_000_000, bytes_accessed=8_000_000, transcendentals=0),
        name="gather",
    )(*(pltpu.with_memory_space_constraint(x, pltpu.HBM) for x in (
        child_pattern,
        child_sources.T,
        child_classes.T,
        child_counts.reshape(4, 128),
        parent_sources,
        parent_classes,
        parent_counts,
        child_table.transpose(1, 2, 3, 0),
        theta_index.T,
        theta_weight.T,
        phi_index.T,
        phi_weight.T,
        shift_angle.reshape(128, 128),
    )))
    child_incoming, pattern, incoming = pl.pallas_call(
        list_kernel,
        out_shape=(
            jax.ShapeDtypeStruct((32, 2, 8, 64), f32),
            jax.ShapeDtypeStruct((128, 128), f32),
            jax.ShapeDtypeStruct((128, 128), f32),
        ),
        in_specs=[vmem] * 4 + [pl.BlockSpec(memory_space=pltpu.SMEM)] * 2 + [vmem],
        out_specs=(hbm, hbm, hbm),
        scratch_shapes=[
            pltpu.VMEM((32, 2, 8, 64), f32),
            pltpu.VMEM((128, 128), f32),
            pltpu.VMEM((2, 32, 8, 128), f32),
            dma((8,)),
        ],
        compiler_params=pltpu.CompilerParams(vmem_limit_bytes=24 * 2**20),
        name="lists",
    )(g, f, acc, pg, ci, pi, parent_table.reshape(CLASSES * 32, 128))
    shape = (4, 2, 16, 128)
    return child_incoming, pattern.reshape(shape), incoming.reshape(shape)


def solution(mesh):
    return jax.shard_map(
        local,
        mesh=mesh,
        in_specs=(
            P("clus", None, "ang", None),
            P(), P(), P(), P(), P(), P(),
            P(None, None, "ang", None),
            P(None, None, "ang", None),
            P(), P(),
            P("ang", None),
            P("ang", None),
            P(None, "ang", None),
        ),
        out_specs=(
            P("clus", None, "ang", None),
            P("clus", None, "ang", None),
            P("clus", None, "ang", None),
        ),
        check_vma=False,
    )
```

```python
import functools

import jax
import jax.numpy as jnp
from jax import lax
from jax.experimental import pallas as pl
from jax.experimental.pallas import tpu as pltpu
from jax.sharding import PartitionSpec as P

MESH = pl.DeviceIdType.MESH
SLOTS = 189
CLASSES = 316
HEAD = 32
CHILD_TAIL = 25
PARENT_TAIL = 27
CHUNKS = 2


def rows_at(start, size):
    return pl.ds(pl.multiple_of(start, 8), size)


def gather_kernel(
    pat_hbm, cs_hbm, cc_hbm, ccnt_hbm, ps_hbm, pc_hbm, pcnt_hbm, tab_hbm,
    thi_hbm, thw_hbm, phi_hbm, phw_hbm, ang_hbm,
    g_ref, f_ref, acc_ref, pg_ref, ci_ref, pi_ref,
    pat, sv, cv, ccnt, psv, pcv, pcnt, tab, thi, thw, phi, phw, ang,
    own, hs, hr, zs, pair, turns, pv, ta, sa_s, sa_c,
    loc, smsem, hsend, hrecv, csend, crecv, cssend, csrecv, psend, precv,
):
    r = lax.axis_index("clus")
    a = lax.axis_index("ang")
    sib = r + 1 - 2 * lax.rem(r, 2)
    up, down = lax.rem(r + 2, 16), lax.rem(r + 14, 16)
    ahead, behind = lax.rem(a + 1, 16), lax.rem(a + 15, 16)

    barrier = pltpu.get_barrier_semaphore()
    for target in (up, down, sib):
        pl.semaphore_signal(barrier, inc=1, device_id={"clus": target}, device_id_type=MESH)
    for target in (ahead, behind):
        pl.semaphore_signal(barrier, inc=1, device_id={"ang": target}, device_id_type=MESH)

    lane_block = pl.ds(pl.multiple_of(lax.div(r, 4) * 128, 128), 128)
    row_block = rows_at(lax.div(r, 2) * 8, 8)
    locals_ = [
        (pat_hbm, pat),
        (cs_hbm.at[:, lane_block], sv),
        (cc_hbm.at[:, lane_block], cv),
        (ccnt_hbm, ccnt),
        (ps_hbm.at[row_block, :], psv),
        (pc_hbm.at[row_block, :], pcv),
        (pcnt_hbm, pcnt),
        (thi_hbm, thi),
        (thw_hbm, thw),
        (phi_hbm, phi),
        (phw_hbm, phw),
        (ang_hbm, ang),
        (tab_hbm, tab),
    ]
    copies = [pltpu.make_async_copy(src, dst, loc.at[i]) for i, (src, dst) in enumerate(locals_)]
    for copy in copies:
        copy.start()

    pl.semaphore_wait(barrier, 5)

    def mover(buffer, block_rows, send, recv, sib_send, sib_recv):
        size = block_rows // CHUNKS

        def part(owner, ch):
            return buffer.at[rows_at(owner * block_rows + ch * size, size), :]

        def ring(way, step, ch):
            back = 16 - 2 * (step - 1) if way == 0 else 2 * (step - 1)
            block = part(lax.rem(r + back, 16), ch)
            k = (8 - step) if way == 0 else step
            return pltpu.make_async_remote_copy(
                src_ref=block, dst_ref=block,
                send_sem=send.at[way, step - 1, ch], recv_sem=recv.at[k, ch],
                device_id={"clus": up if way == 0 else down}, device_id_type=MESH,
            )

        def arrived(way, step, ch):
            k = (8 - step) if way == 0 else step
            block = part(lax.rem(r + 2 * k, 16), ch)
            pltpu.make_async_remote_copy(
                src_ref=block, dst_ref=block,
                send_sem=send.at[way, step - 1, ch], recv_sem=recv.at[k, ch],
                device_id={"clus": up if way == 0 else down}, device_id_type=MESH,
            ).wait_recv()

        def side(k, ch, mine=True):
            block = part(lax.rem((r if mine else sib) + 2 * k, 16), ch)
            return pltpu.make_async_remote_copy(
                src_ref=block, dst_ref=block,
                send_sem=sib_send.at[k, ch], recv_sem=sib_recv.at[k, ch],
                device_id={"clus": sib}, device_id_type=MESH,
            )

        def uses(way, step, ch):
            return step < 4 or (ch < CHUNKS // 2) == (way == 0)

        def first(ch):
            for way in (0, 1):
                ring(way, 1, ch).start()
            side(0, ch).start()

        def onward(step, ch):
            for way in (0, 1):
                if uses(way, step, ch):
                    arrived(way, step, ch)
                    if step < 4 and uses(way, step + 1, ch):
                        ring(way, step + 1, ch).start()
                    side((8 - step) if way == 0 else step, ch).start()

        def landed(places):
            for k in places:
                for ch in range(CHUNKS):
                    side(k, ch, mine=False).wait_recv()

        def drained(steps, places):
            for ch in range(CHUNKS):
                for step in steps:
                    for way in (0, 1):
                        if uses(way, step, ch):
                            ring(way, step, ch).wait_send()
                for k in places:
                    side(k, ch).wait_send()

        return first, onward, landed, drained

    c_first, c_onward, c_landed, c_drained = mover(g_ref, 256, csend, crecv, cssend, csrecv)

    copies[0].wait()
    size = 32 // CHUNKS
    for ch in range(CHUNKS):
        x = pat[ch * size:(ch + 1) * size]
        x = jnp.concatenate([x[:, 0], x[:, 1]], axis=2).reshape(size * 8, 128)
        own[ch * size * 8:(ch + 1) * size * 8, :] = x
        g_ref[rows_at(r * 256 + ch * size * 8, size * 8), :] = x
        c_first(ch)

    def edge(k, way):
        return pltpu.make_async_remote_copy(
            src_ref=hs.at[k, way], dst_ref=hr.at[k, way], send_sem=hsend.at[k, way], recv_sem=hrecv.at[k, way],
            device_id={"ang": ahead if way == 0 else behind}, device_id_type=MESH,
        )

    def owner(k):
        return lax.rem(r + 2 * k, 16)

    def edges(k):
        own[...] = g_ref[rows_at(owner(k) * 256, 256), :]
        for way in (0, 1):
            for j in range(2):
                hs[k, way, j * 32:(j + 1) * 32, :] = own[pl.ds((6 if way == 0 else 0) + j, 32, stride=8), :]
            edge(k, way).start()

    def aside(k, mine=True):
        block = pg_ref.at[rows_at(lax.rem((r if mine else sib) + 2 * k, 16) * 128, 128), :]
        return pltpu.make_async_remote_copy(
            src_ref=block, dst_ref=block, send_sem=psend.at[k], recv_sem=precv.at[k],
            device_id={"clus": sib}, device_id_type=MESH,
        )

    edges(0)


    for i in (7, 8, 9, 10, 11):
        copies[i].wait()
    row = lax.broadcasted_iota(jnp.int32, (64, 128), 0)
    theta = jnp.zeros((64, 128), jnp.float32)
    for i in range(4):
        theta = theta + jnp.where(thi[i:i + 1, :] == row, thw[i:i + 1, :], 0.0)
    blank = jnp.zeros((64, 128), jnp.float32)
    pair[...] = jnp.concatenate(
        [jnp.concatenate([theta, blank], axis=1), jnp.concatenate([blank, theta], axis=1)], axis=0
    )
    angles = ang[...]
    turns[0] = jnp.cos(angles)
    turns[1] = jnp.sin(angles)
    offset = lax.rem(phi[...] - a * 8 + (2 + 128), 128)
    weights = phw[...]
    base = lax.shift_right_logical(lax.broadcasted_iota(jnp.int32, (1, 16), 1), 1)
    taps = []
    for d in range(5):
        tap = jnp.zeros((1, 16), jnp.float32)
        for i in range(4):
            tap = tap + jnp.where(offset[i:i + 1, :] == base + d, weights[i:i + 1, :], 0.0)
        taps.append(tap)

    def aggregate(k):
        for way in (0, 1):
            edge(k, way).wait_recv()
        own[...] = g_ref[rows_at(owner(k) * 256, 256), :]
        cols = [hr[k, 0, :32, :], hr[k, 0, 32:, :]]
        cols += [own[pl.ds(j, 32, stride=8), :] for j in range(8)]
        cols += [hr[k, 1, :32, :], hr[k, 1, 32:, :]]
        for j in range(16):
            z = jnp.zeros((32, 128), jnp.float32)
            for d in range(5):
                z = z + taps[d][:, j:j + 1] * cols[j // 2 + d]
            zs[pl.ds(j, 32, stride=16), :] = z
        for parent in range(4):
            y = jnp.dot(
                zs[parent * 128:(parent + 1) * 128, :], pair[...],
                precision=lax.Precision.HIGHEST, preferred_element_type=jnp.float32,
            )
            re = y[:, :128] * turns[0] - y[:, 128:] * turns[1]
            im = y[:, :128] * turns[1] + y[:, 128:] * turns[0]
            re = jnp.sum(re.reshape(8, 16, 128), axis=0)
            im = jnp.sum(im.reshape(8, 16, 128), axis=0)
            at = owner(k) * 128 + parent * 32
            pg_ref[rows_at(at, 16), :] = re
            pg_ref[rows_at(at + 16, 16), :] = im
        aside(k).start()

    def pair_of(step):
        def one(i, carry):
            aggregate(8 - step + i * (2 * step - 8))
            return carry

        lax.fori_loop(0, 2, one, 0)

    pg_ref[2048:2080, :] = jnp.zeros((32, 128), jnp.float32)

    for i in (1, 2, 3):
        copies[i].wait()
    count_row = ccnt[pl.ds(lax.div(r, 4), 1), :]
    own_rows = rows_at(lax.rem(r, 4) * 32, 32)
    slot = lax.broadcasted_iota(jnp.int32, (128, 128), 0)

    def lists(start, stop):
        s, c = sv[start:stop, :], cv[start:stop, :]
        live = slot[:stop - start] + start < count_row
        return jnp.where(live, s, 0), jnp.where(live, c, CLASSES)

    s, c = lists(0, 128)
    ta[0] = s.T
    ta[1] = c.T
    fill = [
        pltpu.make_async_copy(ta.at[0, own_rows, :], sa_s, smsem.at[0]),
        pltpu.make_async_copy(ta.at[1, own_rows, :], sa_c, smsem.at[1]),
    ]
    for copy in fill:
        copy.start()

    for half, (begin, end) in enumerate(((HEAD, HEAD + 128), (HEAD + 128, SLOTS))):
        s, c = lists(begin, end)
        s, c = s * 8, c * 16
        if half:
            rest = 128 - (end - begin)
            s = jnp.concatenate([s, jnp.zeros((rest, 128), jnp.int32)], axis=0)
            c = jnp.concatenate([c, jnp.full((rest, 128), CLASSES * 16, jnp.int32)], axis=0)
            c = jnp.where(slot == 127, count_row, c)
        ta[2 + half] = s.T
        ta[4 + half] = c.T
    for i in range(4):
        fill.append(
            pltpu.make_async_copy(ta.at[2 + i, own_rows, :], ci_ref.at[pl.ds(32 * i, 32), :], smsem.at[2 + i])
        )
        fill[2 + i].start()


    c_onward(1, 0)
    c_onward(1, 1)
    edges(7)
    edges(1)

    aggregate(0)

    for i in (4, 5, 6):
        copies[i].wait()
    line = lax.broadcasted_iota(jnp.int32, (8, 128), 0)
    lane = lax.broadcasted_iota(jnp.int32, (8, 128), 1)
    counts = jnp.zeros((8, 128), jnp.int32)
    for i in range(8):
        counts = jnp.where(line == i, pcnt[lax.div(r, 2) * 8 + i], counts)
    pads = jnp.zeros((8, 256 - SLOTS), jnp.int32)
    for half in range(2):
        if half == 0:
            s, c = psv[:, :128], pcv[:, :128]
        else:
            s = jnp.concatenate([psv[:, 128:], pads], axis=1)
            c = jnp.concatenate([pcv[:, 128:], pads], axis=1)
        live = lane + half * 128 < counts
        s = jnp.where(live, s, 64) * 32
        c = jnp.where(live, c, 0) * 32
        pv[half * 8:half * 8 + 8, :] = s
        pv[16 + half * 8:16 + half * 8 + 8, :] = jnp.where(lane == 127, counts, c) if half else c

    fill.append(pltpu.make_async_copy(pv, pi_ref, smsem.at[6]))
    fill[6].start()


    copies[12].wait()

    def operators(col):
        for b in range(3):
            lo, hi = b * 128, min((b + 1) * 128, CLASSES)
            x = jnp.concatenate([tab[0, col, :, lo:hi], tab[1, col, :, lo:hi]], axis=0)
            if hi - lo < 128:
                x = jnp.concatenate([x, jnp.zeros((128, 128 - (hi - lo)), jnp.float32)], axis=1)
            y = x.T
            f_ref[pl.ds(lo * 16 + col, 128, stride=16), :] = y
            f_ref[pl.ds(lo * 16 + col + 8, 128, stride=16), :] = pltpu.roll(y, 64, 1)


    for col in range(4):
        operators(col)

    c_onward(2, 0)
    c_onward(2, 1)
    edges(6)
    edges(2)

    pair_of(1)

    for col in range(4, 8):
        operators(col)

    c_onward(3, 0)
    c_onward(3, 1)
    edges(5)
    edges(3)

    pair_of(2)

    c_drained((1, 2), (0, 7, 1, 6, 2))
    c_landed((0, 7, 1, 6, 2))
    for copy in fill:
        copy.wait()

    c_onward(4, 0)
    c_onward(4, 1)
    edges(4)

    pair_of(3)

    c_landed((5, 3, 4))

    g3, f4 = g_ref.reshape(512, 8, 128), f_ref.reshape(384, 2, 8, 128)

    def head(p, carry):
        zero = jnp.zeros((8, 128), jnp.float32)
        one, two = zero, zero
        for m in range(HEAD):
            s, c = sa_s[p, m], sa_c[p, m]
            x = g3[s]
            one = one + x * f4[c, 0]
            two = two + x * f4[c, 1]
        acc_ref[rows_at(p * 16, 8), :] = one
        acc_ref[rows_at(p * 16 + 8, 8), :] = two

        @pl.when(p == 4)
        def _():
            aggregate(4)

        return carry

    lax.fori_loop(0, 32, head, 0)

    c_drained((3, 4), (5, 3, 4))
    for k in range(8):
        for way in (0, 1):
            edge(k, way).wait_send()
        aside(k, mine=False).wait_recv()
        aside(k).wait_send()


def list_kernel(
    g_ref, f_ref, acc_ref, pg_ref, ci, pi, pt_ref,
    child_out, pattern_out, incoming_out,
    child, incoming, sums, sem,
):
    r = lax.axis_index("clus")
    pattern = pltpu.make_async_copy(pg_ref.at[rows_at(r * 128, 128), :], pattern_out, sem.at[2])
    pattern.start()

    def run(count, width, last, chunk, total, start=0):
        if start >= last:
            return total
        stop = min(start + width, last)

        def more(total):
            return run(count, width, last, chunk, chunk(start, stop, total), stop)

        return lax.cond(count > start, more, lambda total: total, total)

    def parent(p, carry):
        line = lax.rem(r, 2) * 4 + p

        def chunk(start, stop, total):
            re, im = total
            for m in range(start, stop):
                row = line + 8 * (m // 128)
                s = pl.multiple_of(pi[row, m % 128], 32)
                c = pl.multiple_of(pi[16 + row, m % 128], 32)
                sr, si = pg_ref[pl.ds(s, 16), :], pg_ref[pl.ds(s + 16, 16), :]
                tr, ti = pt_ref[pl.ds(c, 16), :], pt_ref[pl.ds(c + 16, 16), :]
                re = re + (sr * tr - si * ti)
                im = im + (sr * ti + si * tr)
            return re, im

        zero = jnp.zeros((16, 128), jnp.float32)
        re, im = run(pi[24 + line, 127], PARENT_TAIL, SLOTS, chunk, (zero, zero))
        incoming[rows_at(p * 32, 16), :] = re
        incoming[rows_at(p * 32 + 16, 16), :] = im
        return carry

    lax.fori_loop(0, 4, parent, 0)
    done = pltpu.make_async_copy(incoming, incoming_out, sem.at[3])
    done.start()

    def tail(p, carry):
        def chunk(start, stop, total):
            one, two = total
            for m in range(start, stop):
                row = p + 32 * (m // 128)
                s = pl.multiple_of(ci[row, m % 128], 8)
                c = pl.multiple_of(ci[64 + row, m % 128], 16)
                x = g_ref[pl.ds(s, 8), :]
                one = one + x * f_ref[pl.ds(c, 8), :]
                two = two + x * f_ref[pl.ds(c + 8, 8), :]
            return one, two

        start = (acc_ref[rows_at(p * 16, 8), :], acc_ref[rows_at(p * 16 + 8, 8), :])
        one, two = run(ci[96 + p, 127] - HEAD, CHILD_TAIL, SLOTS - HEAD, chunk, start)
        sums[0, p] = one
        sums[1, p] = two
        return carry

    parts = []
    for i in range(4):
        lax.fori_loop(8 * i, 8 * i + 8, tail, 0)
        group = pl.ds(8 * i, 8)
        one, two = sums[0, group].reshape(64, 128), sums[1, group].reshape(64, 128)
        re, im = one - pltpu.roll(one, 64, 1), two + pltpu.roll(two, 64, 1)
        child[group, 0] = re[:, :64].reshape(8, 8, 64)
        child[group, 1] = im[:, :64].reshape(8, 8, 64)
        parts.append(pltpu.make_async_copy(child.at[group], child_out.at[group], sem.at[4 + i]))
        parts[i].start()
    pattern.wait()
    done.wait()
    for part in parts:
        part.wait()


def local(
    child_pattern, child_sources, child_classes, child_counts,
    parent_sources, parent_classes, parent_counts,
    child_table, parent_table, theta_index, theta_weight, phi_index, phi_weight, shift_angle,
):
    f32, i32 = jnp.float32, jnp.int32
    hbm = pl.BlockSpec(memory_space=pltpu.HBM)
    vmem = pl.BlockSpec(memory_space=pltpu.VMEM)
    dma = pltpu.SemaphoreType.DMA
    g, f, acc, pg, ci, pi = pl.pallas_call(
        gather_kernel,
        out_shape=(
            jax.ShapeDtypeStruct((4096, 128), f32),
            jax.ShapeDtypeStruct((6144, 128), f32),
            jax.ShapeDtypeStruct((512, 128), f32),
            jax.ShapeDtypeStruct((2080, 128), f32),
            pltpu.SMEM((128, 128), i32),
            pltpu.SMEM((32, 128), i32),
        ),
        in_specs=[hbm] * 13,
        out_specs=(vmem,) * 4 + (pl.BlockSpec(memory_space=pltpu.SMEM),) * 2,
        scratch_shapes=[
            pltpu.VMEM((32, 2, 8, 64), f32),
            pltpu.VMEM((SLOTS, 128), i32),
            pltpu.VMEM((SLOTS, 128), i32),
            pltpu.VMEM((4, 128), i32),
            pltpu.VMEM((8, SLOTS), i32),
            pltpu.VMEM((8, SLOTS), i32),
            pltpu.SMEM((64,), i32),
            pltpu.VMEM((2, 8, 64, CLASSES), f32),
            pltpu.VMEM((4, 128), i32),
            pltpu.VMEM((4, 128), f32),
            pltpu.VMEM((4, 16), i32),
            pltpu.VMEM((4, 16), f32),
            pltpu.VMEM((128, 128), f32),
            pltpu.VMEM((256, 128), f32),
            pltpu.VMEM((8, 2, 64, 128), f32),
            pltpu.VMEM((8, 2, 64, 128), f32),
            pltpu.VMEM((512, 128), f32),
            pltpu.VMEM((128, 256), f32),
            pltpu.VMEM((2, 128, 128), f32),
            pltpu.VMEM((32, 128), i32),
            pltpu.VMEM((6, 128, 128), i32),
            pltpu.SMEM((32, 128), i32),
            pltpu.SMEM((32, 128), i32),
            dma((13,)),
            dma((7,)),
            dma((8, 2)),
            dma((8, 2)),
            dma((2, 4, CHUNKS)),
            dma((8, CHUNKS)),
            dma((8, CHUNKS)),
            dma((8, CHUNKS)),
            dma((8,)),
            dma((8,)),
        ],
        compiler_params=pltpu.CompilerParams(
            collective_id=0, has_side_effects=True, vmem_limit_bytes=24 * 2**20
        ),
        cost_estimate=pl.CostEstimate(flops=30_000_000_000, bytes_accessed=8_000_000, transcendentals=0),
        name="gather",
    )(*(pltpu.with_memory_space_constraint(x, pltpu.HBM) for x in (
        child_pattern,
        child_sources.T,
        child_classes.T,
        child_counts.reshape(4, 128),
        parent_sources,
        parent_classes,
        parent_counts,
        child_table.transpose(1, 2, 3, 0),
        theta_index.T,
        theta_weight.T,
        phi_index.T,
        phi_weight.T,
        shift_angle.reshape(128, 128),
    )))
    child_incoming, pattern, incoming = pl.pallas_call(
        list_kernel,
        out_shape=(
            jax.ShapeDtypeStruct((32, 2, 8, 64), f32),
            jax.ShapeDtypeStruct((128, 128), f32),
            jax.ShapeDtypeStruct((128, 128), f32),
        ),
        in_specs=[vmem] * 4 + [pl.BlockSpec(memory_space=pltpu.SMEM)] * 2 + [vmem],
        out_specs=(hbm, hbm, hbm),
        scratch_shapes=[
            pltpu.VMEM((32, 2, 8, 64), f32),
            pltpu.VMEM((128, 128), f32),
            pltpu.VMEM((2, 32, 8, 128), f32),
            dma((8,)),
        ],
        compiler_params=pltpu.CompilerParams(vmem_limit_bytes=24 * 2**20),
        name="lists",
    )(g, f, acc, pg, ci, pi, parent_table.reshape(CLASSES * 32, 128))
    shape = (4, 2, 16, 128)
    return child_incoming, pattern.reshape(shape), incoming.reshape(shape)


def solution(mesh):
    return jax.shard_map(
        local,
        mesh=mesh,
        in_specs=(
            P("clus", None, "ang", None),
            P(), P(), P(), P(), P(), P(),
            P(None, None, "ang", None),
            P(None, None, "ang", None),
            P(), P(),
            P("ang", None),
            P("ang", None),
            P(None, "ang", None),
        ),
        out_specs=(
            P("clus", None, "ang", None),
            P("clus", None, "ang", None),
            P("clus", None, "ang", None),
        ),
        check_vma=False,
    )
```

```python
import functools

import jax
import jax.numpy as jnp
from jax import lax
from jax.experimental import pallas as pl
from jax.experimental.pallas import tpu as pltpu
from jax.sharding import PartitionSpec as P

MESH = pl.DeviceIdType.MESH
SLOTS = 189
CLASSES = 316
HEAD = 52
CHILD_TAIL = 35
PARENT_TAIL = 27
CHUNKS = 2


def rows_at(start, size):
    return pl.ds(pl.multiple_of(start, 8), size)


def gather_kernel(
    pat_hbm, cs_hbm, cc_hbm, ccnt_hbm, ps_hbm, pc_hbm, pcnt_hbm, tab_hbm,
    thi_hbm, thw_hbm, phi_hbm, phw_hbm, ang_hbm,
    g_ref, f_ref, acc_ref, pg_ref, ci_ref, pi_ref,
    pat, sv, cv, ccnt, psv, pcv, pcnt, tab, thi, thw, phi, phw, ang,
    own, hs, hr, zs, pair, turns, spread, pv, ta, sa_s, sa_c,
    loc, smsem, hsend, hrecv, csend, crecv, cssend, csrecv, psend, precv,
):
    r = lax.axis_index("clus")
    a = lax.axis_index("ang")
    sib = r + 1 - 2 * lax.rem(r, 2)
    up, down = lax.rem(r + 2, 16), lax.rem(r + 14, 16)
    ahead, behind = lax.rem(a + 1, 16), lax.rem(a + 15, 16)

    barrier = pltpu.get_barrier_semaphore()
    for target in (up, down, sib):
        pl.semaphore_signal(barrier, inc=1, device_id={"clus": target}, device_id_type=MESH)
    for target in (ahead, behind):
        pl.semaphore_signal(barrier, inc=1, device_id={"ang": target}, device_id_type=MESH)

    lane_block = pl.ds(pl.multiple_of(lax.div(r, 4) * 128, 128), 128)
    row_block = rows_at(lax.div(r, 2) * 8, 8)
    locals_ = [
        (pat_hbm, pat),
        (cs_hbm.at[:, lane_block], sv),
        (cc_hbm.at[:, lane_block], cv),
        (ccnt_hbm, ccnt),
        (ps_hbm.at[row_block, :], psv),
        (pc_hbm.at[row_block, :], pcv),
        (pcnt_hbm, pcnt),
        (thi_hbm, thi),
        (thw_hbm, thw),
        (phi_hbm, phi),
        (phw_hbm, phw),
        (ang_hbm, ang),
        (tab_hbm, tab),
    ]
    copies = [pltpu.make_async_copy(src, dst, loc.at[i]) for i, (src, dst) in enumerate(locals_)]
    for copy in copies:
        copy.start()

    pl.semaphore_wait(barrier, 5)

    def mover(buffer, block_rows, send, recv, sib_send, sib_recv):
        size = block_rows // CHUNKS

        def part(owner, ch):
            return buffer.at[rows_at(owner * block_rows + ch * size, size), :]

        def ring(way, step, ch):
            back = 16 - 2 * (step - 1) if way == 0 else 2 * (step - 1)
            block = part(lax.rem(r + back, 16), ch)
            k = (8 - step) if way == 0 else step
            return pltpu.make_async_remote_copy(
                src_ref=block, dst_ref=block,
                send_sem=send.at[way, step - 1, ch], recv_sem=recv.at[k, ch],
                device_id={"clus": up if way == 0 else down}, device_id_type=MESH,
            )

        def arrived(way, step, ch):
            k = (8 - step) if way == 0 else step
            block = part(lax.rem(r + 2 * k, 16), ch)
            pltpu.make_async_remote_copy(
                src_ref=block, dst_ref=block,
                send_sem=send.at[way, step - 1, ch], recv_sem=recv.at[k, ch],
                device_id={"clus": up if way == 0 else down}, device_id_type=MESH,
            ).wait_recv()

        def side(k, ch, mine=True):
            block = part(lax.rem((r if mine else sib) + 2 * k, 16), ch)
            return pltpu.make_async_remote_copy(
                src_ref=block, dst_ref=block,
                send_sem=sib_send.at[k, ch], recv_sem=sib_recv.at[k, ch],
                device_id={"clus": sib}, device_id_type=MESH,
            )

        def uses(way, step, ch):
            return step < 4 or (ch < CHUNKS // 2) == (way == 0)

        def first(ch):
            for way in (0, 1):
                ring(way, 1, ch).start()
            side(0, ch).start()

        def onward(step, ch):
            for way in (0, 1):
                if uses(way, step, ch):
                    arrived(way, step, ch)
                    if step < 4 and uses(way, step + 1, ch):
                        ring(way, step + 1, ch).start()
                    side((8 - step) if way == 0 else step, ch).start()

        def landed(places):
            for k in places:
                for ch in range(CHUNKS):
                    side(k, ch, mine=False).wait_recv()

        def drained(steps, places):
            for ch in range(CHUNKS):
                for step in steps:
                    for way in (0, 1):
                        if uses(way, step, ch):
                            ring(way, step, ch).wait_send()
                for k in places:
                    side(k, ch).wait_send()

        return first, onward, landed, drained

    c_first, c_onward, c_landed, c_drained = mover(g_ref, 256, csend, crecv, cssend, csrecv)

    copies[0].wait()
    size = 32 // CHUNKS
    for ch in range(CHUNKS):
        x = pat[ch * size:(ch + 1) * size]
        x = jnp.concatenate([x[:, 0], x[:, 1]], axis=2).reshape(size * 8, 128)
        own[ch * size * 8:(ch + 1) * size * 8, :] = x
        g_ref[rows_at(r * 256 + ch * size * 8, size * 8), :] = x
        c_first(ch)

    def edge(k, way):
        return pltpu.make_async_remote_copy(
            src_ref=hs.at[k, way], dst_ref=hr.at[k, way], send_sem=hsend.at[k, way], recv_sem=hrecv.at[k, way],
            device_id={"ang": ahead if way == 0 else behind}, device_id_type=MESH,
        )

    def owner(k):
        return lax.rem(r + 2 * k, 16)

    def edges(k):
        own[...] = g_ref[rows_at(owner(k) * 256, 256), :]
        for way in (0, 1):
            for j in range(2):
                hs[k, way, j * 32:(j + 1) * 32, :] = own[pl.ds((6 if way == 0 else 0) + j, 32, stride=8), :]
            edge(k, way).start()

    def aside(k, mine=True):
        block = pg_ref.at[rows_at(lax.rem((r if mine else sib) + 2 * k, 16) * 128, 128), :]
        return pltpu.make_async_remote_copy(
            src_ref=block, dst_ref=block, send_sem=psend.at[k], recv_sem=precv.at[k],
            device_id={"clus": sib}, device_id_type=MESH,
        )

    edges(0)


    for i in (7, 8, 9, 10, 11):
        copies[i].wait()
    row = lax.broadcasted_iota(jnp.int32, (64, 128), 0)
    theta = jnp.zeros((64, 128), jnp.float32)
    for i in range(4):
        theta = theta + jnp.where(thi[i:i + 1, :] == row, thw[i:i + 1, :], 0.0)
    blank = jnp.zeros((64, 128), jnp.float32)
    pair[...] = jnp.concatenate(
        [jnp.concatenate([theta, blank], axis=1), jnp.concatenate([blank, theta], axis=1)], axis=0
    )
    angles = ang[...]
    turns[0] = jnp.cos(angles)
    turns[1] = jnp.sin(angles)
    offset = lax.rem(phi[...] - a * 8 + (2 + 128), 128)
    weights = phw[...]
    base = lax.shift_right_logical(lax.broadcasted_iota(jnp.int32, (1, 16), 1), 1)
    taps = []
    for d in range(5):
        tap = jnp.zeros((1, 16), jnp.float32)
        for i in range(4):
            tap = tap + jnp.where(offset[i:i + 1, :] == base + d, weights[i:i + 1, :], 0.0)
        taps.append(tap)

    for j in range(16):
        for d in range(5):
            spread[5 * j + d] = jnp.broadcast_to(taps[d][:, j:j + 1], (8, 128))

    def aggregate(k):
        for way in (0, 1):
            edge(k, way).wait_recv()
        own[...] = g_ref[rows_at(owner(k) * 256, 256), :]
        cols = [hr[k, 0, :32, :], hr[k, 0, 32:, :]]
        cols += [own[pl.ds(j, 32, stride=8), :] for j in range(8)]
        cols += [hr[k, 1, :32, :], hr[k, 1, 32:, :]]
        cols = [x.reshape(4, 8, 128) for x in cols]
        for j in range(16):
            z = cols[j // 2] * spread[5 * j]
            for d in range(1, 5):
                z = z + cols[j // 2 + d] * spread[5 * j + d]
            zs[pl.ds(j, 32, stride=16), :] = z.reshape(32, 128)
        for parent in range(4):
            y = jnp.dot(
                zs[parent * 128:(parent + 1) * 128, :], pair[...],
                precision=lax.Precision.HIGHEST, preferred_element_type=jnp.float32,
            )
            re = y[:, :128] * turns[0] - y[:, 128:] * turns[1]
            im = y[:, :128] * turns[1] + y[:, 128:] * turns[0]
            re = jnp.sum(re.reshape(8, 16, 128), axis=0)
            im = jnp.sum(im.reshape(8, 16, 128), axis=0)
            at = owner(k) * 128 + parent * 32
            pg_ref[rows_at(at, 16), :] = re
            pg_ref[rows_at(at + 16, 16), :] = im
        aside(k).start()

    def pair_of(step):
        def one(i, carry):
            aggregate(8 - step + i * (2 * step - 8))
            return carry

        lax.fori_loop(0, 2, one, 0)

    pg_ref[2048:2080, :] = jnp.zeros((32, 128), jnp.float32)

    for i in (1, 2, 3):
        copies[i].wait()
    count_row = ccnt[pl.ds(lax.div(r, 4), 1), :]
    own_rows = rows_at(lax.rem(r, 4) * 32, 32)
    slot = lax.broadcasted_iota(jnp.int32, (128, 128), 0)

    def lists(start, stop):
        s, c = sv[start:stop, :], cv[start:stop, :]
        live = slot[:stop - start] + start < count_row
        return jnp.where(live, s, 0), jnp.where(live, c, CLASSES)

    s, c = lists(0, 128)
    ta[0] = s.T
    ta[1] = c.T
    fill = [
        pltpu.make_async_copy(ta.at[0, own_rows, :], sa_s, smsem.at[0]),
        pltpu.make_async_copy(ta.at[1, own_rows, :], sa_c, smsem.at[1]),
    ]
    for copy in fill:
        copy.start()

    for half, (begin, end) in enumerate(((HEAD, HEAD + 128), (HEAD + 128, SLOTS))):
        s, c = lists(begin, end)
        s, c = s * 8, c * 16
        if half:
            rest = 128 - (end - begin)
            s = jnp.concatenate([s, jnp.zeros((rest, 128), jnp.int32)], axis=0)
            c = jnp.concatenate([c, jnp.full((rest, 128), CLASSES * 16, jnp.int32)], axis=0)
            c = jnp.where(slot == 127, count_row, c)
        ta[2 + half] = s.T
        ta[4 + half] = c.T
    for i in range(4):
        fill.append(
            pltpu.make_async_copy(ta.at[2 + i, own_rows, :], ci_ref.at[pl.ds(32 * i, 32), :], smsem.at[2 + i])
        )
        fill[2 + i].start()


    c_onward(1, 0)
    c_onward(1, 1)
    edges(7)
    edges(1)

    aggregate(0)

    for i in (4, 5, 6):
        copies[i].wait()
    line = lax.broadcasted_iota(jnp.int32, (8, 128), 0)
    lane = lax.broadcasted_iota(jnp.int32, (8, 128), 1)
    counts = jnp.zeros((8, 128), jnp.int32)
    for i in range(8):
        counts = jnp.where(line == i, pcnt[lax.div(r, 2) * 8 + i], counts)
    pads = jnp.zeros((8, 256 - SLOTS), jnp.int32)
    for half in range(2):
        if half == 0:
            s, c = psv[:, :128], pcv[:, :128]
        else:
            s = jnp.concatenate([psv[:, 128:], pads], axis=1)
            c = jnp.concatenate([pcv[:, 128:], pads], axis=1)
        live = lane + half * 128 < counts
        s = jnp.where(live, s, 64) * 32
        c = jnp.where(live, c, 0) * 32
        pv[half * 8:half * 8 + 8, :] = s
        pv[16 + half * 8:16 + half * 8 + 8, :] = jnp.where(lane == 127, counts, c) if half else c

    fill.append(pltpu.make_async_copy(pv, pi_ref, smsem.at[6]))
    fill[6].start()


    copies[12].wait()

    def operators(col):
        for b in range(3):
            lo, hi = b * 128, min((b + 1) * 128, CLASSES)
            x = jnp.concatenate([tab[0, col, :, lo:hi], tab[1, col, :, lo:hi]], axis=0)
            if hi - lo < 128:
                x = jnp.concatenate([x, jnp.zeros((128, 128 - (hi - lo)), jnp.float32)], axis=1)
            y = x.T
            f_ref[pl.ds(lo * 16 + col, 128, stride=16), :] = y
            f_ref[pl.ds(lo * 16 + col + 8, 128, stride=16), :] = pltpu.roll(y, 64, 1)


    for col in range(4):
        operators(col)

    c_onward(2, 0)
    c_onward(2, 1)
    edges(6)
    edges(2)

    pair_of(1)

    for col in range(4, 8):
        operators(col)

    c_onward(3, 0)
    c_onward(3, 1)
    edges(5)
    edges(3)

    pair_of(2)

    c_drained((1, 2), (0, 7, 1, 6, 2))
    c_landed((0, 7, 1, 6, 2))
    for copy in fill:
        copy.wait()

    c_onward(4, 0)
    c_onward(4, 1)
    edges(4)

    pair_of(3)

    c_landed((5, 3, 4))

    g3, f4 = g_ref.reshape(512, 8, 128), f_ref.reshape(384, 2, 8, 128)

    def head(p, carry):
        zero = jnp.zeros((8, 128), jnp.float32)
        one, two = zero, zero
        for m in range(HEAD):
            s, c = sa_s[p, m], sa_c[p, m]
            x = g3[s]
            one = one + x * f4[c, 0]
            two = two + x * f4[c, 1]
        acc_ref[rows_at(p * 16, 8), :] = one
        acc_ref[rows_at(p * 16 + 8, 8), :] = two

        @pl.when(p == 4)
        def _():
            aggregate(4)

        return carry

    lax.fori_loop(0, 32, head, 0)

    c_drained((3, 4), (5, 3, 4))
    for k in range(8):
        for way in (0, 1):
            edge(k, way).wait_send()
        aside(k, mine=False).wait_recv()
        aside(k).wait_send()


def list_kernel(
    g_ref, f_ref, acc_ref, pg_ref, ci, pi, pt_ref,
    child_out, pattern_out, incoming_out,
    child, incoming, sums, sem,
):
    r = lax.axis_index("clus")
    pattern = pltpu.make_async_copy(pg_ref.at[rows_at(r * 128, 128), :], pattern_out, sem.at[2])
    pattern.start()

    def run(count, width, last, chunk, total, start=0):
        if start >= last:
            return total
        stop = min(start + width, last)

        def more(total):
            return run(count, width, last, chunk, chunk(start, stop, total), stop)

        return lax.cond(count > start, more, lambda total: total, total)

    def parent(p, carry):
        line = lax.rem(r, 2) * 4 + p

        def chunk(start, stop, total):
            re, im = total
            for m in range(start, stop):
                row = line + 8 * (m // 128)
                s = pl.multiple_of(pi[row, m % 128], 32)
                c = pl.multiple_of(pi[16 + row, m % 128], 32)
                sr, si = pg_ref[pl.ds(s, 16), :], pg_ref[pl.ds(s + 16, 16), :]
                tr, ti = pt_ref[pl.ds(c, 16), :], pt_ref[pl.ds(c + 16, 16), :]
                re = re + (sr * tr - si * ti)
                im = im + (sr * ti + si * tr)
            return re, im

        zero = jnp.zeros((16, 128), jnp.float32)
        re, im = run(pi[24 + line, 127], PARENT_TAIL, SLOTS, chunk, (zero, zero))
        incoming[rows_at(p * 32, 16), :] = re
        incoming[rows_at(p * 32 + 16, 16), :] = im
        return carry

    lax.fori_loop(0, 4, parent, 0)
    done = pltpu.make_async_copy(incoming, incoming_out, sem.at[3])
    done.start()

    def tail(p, carry):
        def chunk(start, stop, total):
            one, two = total
            for m in range(start, stop):
                row = p + 32 * (m // 128)
                s = pl.multiple_of(ci[row, m % 128], 8)
                c = pl.multiple_of(ci[64 + row, m % 128], 16)
                x = g_ref[pl.ds(s, 8), :]
                one = one + x * f_ref[pl.ds(c, 8), :]
                two = two + x * f_ref[pl.ds(c + 8, 8), :]
            return one, two

        start = (acc_ref[rows_at(p * 16, 8), :], acc_ref[rows_at(p * 16 + 8, 8), :])
        one, two = run(ci[96 + p, 127] - HEAD, CHILD_TAIL, SLOTS - HEAD, chunk, start)
        sums[0, p] = one
        sums[1, p] = two
        return carry

    parts = []
    for i in range(4):
        lax.fori_loop(8 * i, 8 * i + 8, tail, 0)
        group = pl.ds(8 * i, 8)
        one, two = sums[0, group].reshape(64, 128), sums[1, group].reshape(64, 128)
        re, im = one - pltpu.roll(one, 64, 1), two + pltpu.roll(two, 64, 1)
        child[group, 0] = re[:, :64].reshape(8, 8, 64)
        child[group, 1] = im[:, :64].reshape(8, 8, 64)
        parts.append(pltpu.make_async_copy(child.at[group], child_out.at[group], sem.at[4 + i]))
        parts[i].start()
    pattern.wait()
    done.wait()
    for part in parts:
        part.wait()


def local(
    child_pattern, child_sources, child_classes, child_counts,
    parent_sources, parent_classes, parent_counts,
    child_table, parent_table, theta_index, theta_weight, phi_index, phi_weight, shift_angle,
):
    f32, i32 = jnp.float32, jnp.int32
    hbm = pl.BlockSpec(memory_space=pltpu.HBM)
    vmem = pl.BlockSpec(memory_space=pltpu.VMEM)
    dma = pltpu.SemaphoreType.DMA
    g, f, acc, pg, ci, pi = pl.pallas_call(
        gather_kernel,
        out_shape=(
            jax.ShapeDtypeStruct((4096, 128), f32),
            jax.ShapeDtypeStruct((6144, 128), f32),
            jax.ShapeDtypeStruct((512, 128), f32),
            jax.ShapeDtypeStruct((2080, 128), f32),
            pltpu.SMEM((128, 128), i32),
            pltpu.SMEM((32, 128), i32),
        ),
        in_specs=[hbm] * 13,
        out_specs=(vmem,) * 4 + (pl.BlockSpec(memory_space=pltpu.SMEM),) * 2,
        scratch_shapes=[
            pltpu.VMEM((32, 2, 8, 64), f32),
            pltpu.VMEM((SLOTS, 128), i32),
            pltpu.VMEM((SLOTS, 128), i32),
            pltpu.VMEM((4, 128), i32),
            pltpu.VMEM((8, SLOTS), i32),
            pltpu.VMEM((8, SLOTS), i32),
            pltpu.SMEM((64,), i32),
            pltpu.VMEM((2, 8, 64, CLASSES), f32),
            pltpu.VMEM((4, 128), i32),
            pltpu.VMEM((4, 128), f32),
            pltpu.VMEM((4, 16), i32),
            pltpu.VMEM((4, 16), f32),
            pltpu.VMEM((128, 128), f32),
            pltpu.VMEM((256, 128), f32),
            pltpu.VMEM((8, 2, 64, 128), f32),
            pltpu.VMEM((8, 2, 64, 128), f32),
            pltpu.VMEM((512, 128), f32),
            pltpu.VMEM((128, 256), f32),
            pltpu.VMEM((2, 128, 128), f32),
            pltpu.VMEM((80, 8, 128), f32),
            pltpu.VMEM((32, 128), i32),
            pltpu.VMEM((6, 128, 128), i32),
            pltpu.SMEM((32, 128), i32),
            pltpu.SMEM((32, 128), i32),
            dma((13,)),
            dma((7,)),
            dma((8, 2)),
            dma((8, 2)),
            dma((2, 4, CHUNKS)),
            dma((8, CHUNKS)),
            dma((8, CHUNKS)),
            dma((8, CHUNKS)),
            dma((8,)),
            dma((8,)),
        ],
        compiler_params=pltpu.CompilerParams(
            collective_id=0, has_side_effects=True, vmem_limit_bytes=24 * 2**20
        ),
        cost_estimate=pl.CostEstimate(flops=30_000_000_000, bytes_accessed=8_000_000, transcendentals=0),
        name="gather",
    )(*(pltpu.with_memory_space_constraint(x, pltpu.HBM) for x in (
        child_pattern,
        child_sources.T,
        child_classes.T,
        child_counts.reshape(4, 128),
        parent_sources,
        parent_classes,
        parent_counts,
        child_table.transpose(1, 2, 3, 0),
        theta_index.T,
        theta_weight.T,
        phi_index.T,
        phi_weight.T,
        shift_angle.reshape(128, 128),
    )))
    child_incoming, pattern, incoming = pl.pallas_call(
        list_kernel,
        out_shape=(
            jax.ShapeDtypeStruct((32, 2, 8, 64), f32),
            jax.ShapeDtypeStruct((128, 128), f32),
            jax.ShapeDtypeStruct((128, 128), f32),
        ),
        in_specs=[vmem] * 4 + [pl.BlockSpec(memory_space=pltpu.SMEM)] * 2 + [vmem],
        out_specs=(hbm, hbm, hbm),
        scratch_shapes=[
            pltpu.VMEM((32, 2, 8, 64), f32),
            pltpu.VMEM((128, 128), f32),
            pltpu.VMEM((2, 32, 8, 128), f32),
            dma((8,)),
        ],
        compiler_params=pltpu.CompilerParams(vmem_limit_bytes=24 * 2**20),
        name="lists",
    )(g, f, acc, pg, ci, pi, parent_table.reshape(CLASSES * 32, 128))
    shape = (4, 2, 16, 128)
    return child_incoming, pattern.reshape(shape), incoming.reshape(shape)


def solution(mesh):
    return jax.shard_map(
        local,
        mesh=mesh,
        in_specs=(
            P("clus", None, "ang", None),
            P(), P(), P(), P(), P(), P(),
            P(None, None, "ang", None),
            P(None, None, "ang", None),
            P(), P(),
            P("ang", None),
            P("ang", None),
            P(None, "ang", None),
        ),
        out_specs=(
            P("clus", None, "ang", None),
            P("clus", None, "ang", None),
            P("clus", None, "ang", None),
        ),
        check_vma=False,
    )
```

```python
import functools

import jax
import jax.numpy as jnp
from jax import lax
from jax.experimental import pallas as pl
from jax.experimental.pallas import tpu as pltpu
from jax.sharding import PartitionSpec as P

MESH = pl.DeviceIdType.MESH
SLOTS = 189
CLASSES = 316
HEAD = 52
CHILD_TAIL = 35
PARENT_TAIL = 27
CHUNKS = 2


def rows_at(start, size):
    return pl.ds(pl.multiple_of(start, 8), size)


def gather_kernel(
    pat_hbm, cs_hbm, cc_hbm, ccnt_hbm, ps_hbm, pc_hbm, pcnt_hbm, tab_hbm,
    thi_hbm, thw_hbm, phi_hbm, phw_hbm, ang_hbm,
    g_ref, f_ref, acc_ref, pg_ref, ci_ref, pi_ref,
    pat, sv, cv, ccnt, psv, pcv, pcnt, tab, thi, thw, phi, phw, ang,
    own, hs, hr, zs, pair, turns, spread, pv, ta, sa_s, sa_c,
    loc, smsem, hsend, hrecv, csend, crecv, cssend, csrecv, psend, precv,
):
    r = lax.axis_index("clus")
    a = lax.axis_index("ang")
    sib = r + 1 - 2 * lax.rem(r, 2)
    up, down = lax.rem(r + 2, 16), lax.rem(r + 14, 16)
    ahead, behind = lax.rem(a + 1, 16), lax.rem(a + 15, 16)

    barrier = pltpu.get_barrier_semaphore()
    for target in (up, down, sib):
        pl.semaphore_signal(barrier, inc=1, device_id={"clus": target}, device_id_type=MESH)
    for target in (ahead, behind):
        pl.semaphore_signal(barrier, inc=1, device_id={"ang": target}, device_id_type=MESH)

    lane_block = pl.ds(pl.multiple_of(lax.div(r, 4) * 128, 128), 128)
    row_block = rows_at(lax.div(r, 2) * 8, 8)
    locals_ = [
        (pat_hbm, pat),
        (cs_hbm.at[:, lane_block], sv),
        (cc_hbm.at[:, lane_block], cv),
        (ccnt_hbm, ccnt),
        (ps_hbm.at[row_block, :], psv),
        (pc_hbm.at[row_block, :], pcv),
        (pcnt_hbm, pcnt),
        (thi_hbm, thi),
        (thw_hbm, thw),
        (phi_hbm, phi),
        (phw_hbm, phw),
        (ang_hbm, ang),
        (tab_hbm, tab),
    ]
    copies = [pltpu.make_async_copy(src, dst, loc.at[i]) for i, (src, dst) in enumerate(locals_)]
    for copy in copies:
        copy.start()

    pl.semaphore_wait(barrier, 5)

    def mover(buffer, block_rows, send, recv, sib_send, sib_recv):
        size = block_rows // CHUNKS

        def part(owner, ch):
            return buffer.at[rows_at(owner * block_rows + ch * size, size), :]

        def ring(way, step, ch):
            back = 16 - 2 * (step - 1) if way == 0 else 2 * (step - 1)
            block = part(lax.rem(r + back, 16), ch)
            k = (8 - step) if way == 0 else step
            return pltpu.make_async_remote_copy(
                src_ref=block, dst_ref=block,
                send_sem=send.at[way, step - 1, ch], recv_sem=recv.at[k, ch],
                device_id={"clus": up if way == 0 else down}, device_id_type=MESH,
            )

        def arrived(way, step, ch):
            k = (8 - step) if way == 0 else step
            block = part(lax.rem(r + 2 * k, 16), ch)
            pltpu.make_async_remote_copy(
                src_ref=block, dst_ref=block,
                send_sem=send.at[way, step - 1, ch], recv_sem=recv.at[k, ch],
                device_id={"clus": up if way == 0 else down}, device_id_type=MESH,
            ).wait_recv()

        def side(k, ch, mine=True):
            block = part(lax.rem((r if mine else sib) + 2 * k, 16), ch)
            return pltpu.make_async_remote_copy(
                src_ref=block, dst_ref=block,
                send_sem=sib_send.at[k, ch], recv_sem=sib_recv.at[k, ch],
                device_id={"clus": sib}, device_id_type=MESH,
            )

        def uses(way, step, ch):
            return step < 4 or (ch < CHUNKS // 2) == (way == 0)

        def first(ch):
            for way in (0, 1):
                ring(way, 1, ch).start()
            side(0, ch).start()

        def onward(step, ch):
            for way in (0, 1):
                if uses(way, step, ch):
                    arrived(way, step, ch)
                    if step < 4 and uses(way, step + 1, ch):
                        ring(way, step + 1, ch).start()
                    side((8 - step) if way == 0 else step, ch).start()

        def landed(places):
            for k in places:
                for ch in range(CHUNKS):
                    side(k, ch, mine=False).wait_recv()

        def drained(steps, places):
            for ch in range(CHUNKS):
                for step in steps:
                    for way in (0, 1):
                        if uses(way, step, ch):
                            ring(way, step, ch).wait_send()
                for k in places:
                    side(k, ch).wait_send()

        return first, onward, landed, drained

    c_first, c_onward, c_landed, c_drained = mover(g_ref, 256, csend, crecv, cssend, csrecv)

    copies[0].wait()
    size = 32 // CHUNKS
    for ch in range(CHUNKS):
        x = pat[ch * size:(ch + 1) * size]
        x = jnp.concatenate([x[:, 0], x[:, 1]], axis=2).reshape(size * 8, 128)
        own[ch * size * 8:(ch + 1) * size * 8, :] = x
        g_ref[rows_at(r * 256 + ch * size * 8, size * 8), :] = x
        c_first(ch)

    def edge(k, way):
        return pltpu.make_async_remote_copy(
            src_ref=hs.at[k, way], dst_ref=hr.at[k, way], send_sem=hsend.at[k, way], recv_sem=hrecv.at[k, way],
            device_id={"ang": ahead if way == 0 else behind}, device_id_type=MESH,
        )

    def owner(k):
        return lax.rem(r + 2 * k, 16)

    def edges(k):
        own[...] = g_ref[rows_at(owner(k) * 256, 256), :]
        for way in (0, 1):
            for j in range(2):
                hs[k, way, j * 32:(j + 1) * 32, :] = own[pl.ds((6 if way == 0 else 0) + j, 32, stride=8), :]
            edge(k, way).start()

    def aside(k, mine=True):
        block = pg_ref.at[rows_at(lax.rem((r if mine else sib) + 2 * k, 16) * 128, 128), :]
        return pltpu.make_async_remote_copy(
            src_ref=block, dst_ref=block, send_sem=psend.at[k], recv_sem=precv.at[k],
            device_id={"clus": sib}, device_id_type=MESH,
        )

    edges(0)


    for i in (7, 8, 9, 10, 11):
        copies[i].wait()
    row = lax.broadcasted_iota(jnp.int32, (64, 128), 0)
    theta = jnp.zeros((64, 128), jnp.float32)
    for i in range(4):
        theta = theta + jnp.where(thi[i:i + 1, :] == row, thw[i:i + 1, :], 0.0)
    blank = jnp.zeros((64, 128), jnp.float32)
    pair[...] = jnp.concatenate(
        [jnp.concatenate([theta, blank], axis=1), jnp.concatenate([blank, theta], axis=1)], axis=0
    )
    angles = ang[...]
    turns[0] = jnp.cos(angles)
    turns[1] = jnp.sin(angles)
    offset = lax.rem(phi[...] - a * 8 + (2 + 128), 128)
    weights = phw[...]
    base = lax.shift_right_logical(lax.broadcasted_iota(jnp.int32, (1, 16), 1), 1)
    taps = []
    for d in range(5):
        tap = jnp.zeros((1, 16), jnp.float32)
        for i in range(4):
            tap = tap + jnp.where(offset[i:i + 1, :] == base + d, weights[i:i + 1, :], 0.0)
        taps.append(tap)

    for j in range(16):
        for d in range(5):
            spread[5 * j + d] = jnp.broadcast_to(taps[d][:, j:j + 1], (8, 128))

    def aggregate(k):
        for way in (0, 1):
            edge(k, way).wait_recv()
        own[...] = g_ref[rows_at(owner(k) * 256, 256), :]
        cols = [hr[k, 0, :32, :], hr[k, 0, 32:, :]]
        cols += [own[pl.ds(j, 32, stride=8), :] for j in range(8)]
        cols += [hr[k, 1, :32, :], hr[k, 1, 32:, :]]
        cols = [x.reshape(4, 8, 128) for x in cols]
        for j in range(16):
            z = cols[j // 2] * spread[5 * j]
            for d in range(1, 5):
                z = z + cols[j // 2 + d] * spread[5 * j + d]
            zs[pl.ds(j, 32, stride=16), :] = z.reshape(32, 128)
        for parent in range(4):
            y = jnp.dot(
                zs[parent * 128:(parent + 1) * 128, :], pair[...],
                precision=lax.Precision.HIGHEST, preferred_element_type=jnp.float32,
            )
            re = y[:, :128] * turns[0] - y[:, 128:] * turns[1]
            im = y[:, :128] * turns[1] + y[:, 128:] * turns[0]
            re = jnp.sum(re.reshape(8, 16, 128), axis=0)
            im = jnp.sum(im.reshape(8, 16, 128), axis=0)
            at = owner(k) * 128 + parent * 32
            pg_ref[rows_at(at, 16), :] = re
            pg_ref[rows_at(at + 16, 16), :] = im
        aside(k).start()

    def pair_of(step):
        def one(i, carry):
            aggregate(8 - step + i * (2 * step - 8))
            return carry

        lax.fori_loop(0, 2, one, 0)

    pg_ref[2048:2080, :] = jnp.zeros((32, 128), jnp.float32)

    for i in (1, 2, 3):
        copies[i].wait()
    count_row = ccnt[pl.ds(lax.div(r, 4), 1), :]
    own_rows = rows_at(lax.rem(r, 4) * 32, 32)
    slot = lax.broadcasted_iota(jnp.int32, (128, 128), 0)

    def lists(start, stop):
        s, c = sv[start:stop, :], cv[start:stop, :]
        live = slot[:stop - start] + start < count_row
        return jnp.where(live, s, 0), jnp.where(live, c, CLASSES)

    s, c = lists(0, 128)
    ta[0] = s.T
    ta[1] = c.T
    fill = [
        pltpu.make_async_copy(ta.at[0, own_rows, :], sa_s, smsem.at[0]),
        pltpu.make_async_copy(ta.at[1, own_rows, :], sa_c, smsem.at[1]),
    ]
    for copy in fill:
        copy.start()

    for half, (begin, end) in enumerate(((HEAD, HEAD + 128), (HEAD + 128, SLOTS))):
        s, c = lists(begin, end)
        s, c = s * 8, c * 16
        if half:
            rest = 128 - (end - begin)
            s = jnp.concatenate([s, jnp.zeros((rest, 128), jnp.int32)], axis=0)
            c = jnp.concatenate([c, jnp.full((rest, 128), CLASSES * 16, jnp.int32)], axis=0)
            c = jnp.where(slot == 127, count_row, c)
        ta[2 + half] = s.T
        ta[4 + half] = c.T
    for i in range(4):
        fill.append(
            pltpu.make_async_copy(ta.at[2 + i, own_rows, :], ci_ref.at[pl.ds(32 * i, 32), :], smsem.at[2 + i])
        )
        fill[2 + i].start()


    c_onward(1, 0)
    c_onward(1, 1)
    edges(7)
    edges(1)

    aggregate(0)

    for i in (4, 5, 6):
        copies[i].wait()
    line = lax.broadcasted_iota(jnp.int32, (8, 128), 0)
    lane = lax.broadcasted_iota(jnp.int32, (8, 128), 1)
    counts = jnp.zeros((8, 128), jnp.int32)
    for i in range(8):
        counts = jnp.where(line == i, pcnt[lax.div(r, 2) * 8 + i], counts)
    pads = jnp.zeros((8, 256 - SLOTS), jnp.int32)
    for half in range(2):
        if half == 0:
            s, c = psv[:, :128], pcv[:, :128]
        else:
            s = jnp.concatenate([psv[:, 128:], pads], axis=1)
            c = jnp.concatenate([pcv[:, 128:], pads], axis=1)
        live = lane + half * 128 < counts
        s = jnp.where(live, s, 64) * 32
        c = jnp.where(live, c, 0) * 32
        pv[half * 8:half * 8 + 8, :] = s
        pv[16 + half * 8:16 + half * 8 + 8, :] = jnp.where(lane == 127, counts, c) if half else c

    fill.append(pltpu.make_async_copy(pv, pi_ref, smsem.at[6]))
    fill[6].start()


    copies[12].wait()

    def operators(col):
        for b in range(3):
            lo, hi = b * 128, min((b + 1) * 128, CLASSES)
            x = jnp.concatenate([tab[0, col, :, lo:hi], tab[1, col, :, lo:hi]], axis=0)
            if hi - lo < 128:
                x = jnp.concatenate([x, jnp.zeros((128, 128 - (hi - lo)), jnp.float32)], axis=1)
            y = x.T
            f_ref[pl.ds(lo * 16 + col, 128, stride=16), :] = y
            f_ref[pl.ds(lo * 16 + col + 8, 128, stride=16), :] = pltpu.roll(y, 64, 1)


    for col in range(4):
        operators(col)

    c_onward(2, 0)
    c_onward(2, 1)
    edges(6)
    edges(2)

    pair_of(1)

    for col in range(4, 8):
        operators(col)

    c_onward(3, 0)
    c_onward(3, 1)
    edges(5)
    edges(3)

    pair_of(2)

    c_drained((1, 2), (0, 7, 1, 6, 2))
    c_landed((0, 7, 1, 6, 2))
    for copy in fill:
        copy.wait()

    c_onward(4, 0)
    c_onward(4, 1)
    edges(4)

    pair_of(3)

    c_landed((5, 3, 4))

    g3, f4 = g_ref.reshape(512, 8, 128), f_ref.reshape(384, 2, 8, 128)

    def head(p, carry):
        zero = jnp.zeros((8, 128), jnp.float32)
        one, two = zero, zero
        for m in range(HEAD):
            s, c = sa_s[p, m], sa_c[p, m]
            x = g3[s]
            one = one + x * f4[c, 0]
            two = two + x * f4[c, 1]
        acc_ref[rows_at(p * 16, 8), :] = one
        acc_ref[rows_at(p * 16 + 8, 8), :] = two

        @pl.when(p == 20)
        def _():
            aggregate(4)

        return carry

    lax.fori_loop(0, 32, head, 0)

    c_drained((3, 4), (5, 3, 4))
    for k in range(8):
        for way in (0, 1):
            edge(k, way).wait_send()
        aside(k, mine=False).wait_recv()
        aside(k).wait_send()


def list_kernel(
    g_ref, f_ref, acc_ref, pg_ref, ci, pi, pt_ref,
    child_out, pattern_out, incoming_out,
    child, incoming, sums, sem,
):
    r = lax.axis_index("clus")
    pattern = pltpu.make_async_copy(pg_ref.at[rows_at(r * 128, 128), :], pattern_out, sem.at[2])
    pattern.start()

    def run(count, width, last, chunk, total, start=0):
        if start >= last:
            return total
        stop = min(start + width, last)

        def more(total):
            return run(count, width, last, chunk, chunk(start, stop, total), stop)

        return lax.cond(count > start, more, lambda total: total, total)

    def parent(p, carry):
        line = lax.rem(r, 2) * 4 + p

        def chunk(start, stop, total):
            re, im = total
            for m in range(start, stop):
                row = line + 8 * (m // 128)
                s = pl.multiple_of(pi[row, m % 128], 32)
                c = pl.multiple_of(pi[16 + row, m % 128], 32)
                sr, si = pg_ref[pl.ds(s, 16), :], pg_ref[pl.ds(s + 16, 16), :]
                tr, ti = pt_ref[pl.ds(c, 16), :], pt_ref[pl.ds(c + 16, 16), :]
                re = re + (sr * tr - si * ti)
                im = im + (sr * ti + si * tr)
            return re, im

        zero = jnp.zeros((16, 128), jnp.float32)
        re, im = run(pi[24 + line, 127], PARENT_TAIL, SLOTS, chunk, (zero, zero))
        incoming[rows_at(p * 32, 16), :] = re
        incoming[rows_at(p * 32 + 16, 16), :] = im
        return carry

    lax.fori_loop(0, 4, parent, 0)
    done = pltpu.make_async_copy(incoming, incoming_out, sem.at[3])
    done.start()

    def tail(p, carry):
        def chunk(start, stop, total):
            one, two = total
            for m in range(start, stop):
                row = p + 32 * (m // 128)
                s = pl.multiple_of(ci[row, m % 128], 8)
                c = pl.multiple_of(ci[64 + row, m % 128], 16)
                x = g_ref[pl.ds(s, 8), :]
                one = one + x * f_ref[pl.ds(c, 8), :]
                two = two + x * f_ref[pl.ds(c + 8, 8), :]
            return one, two

        start = (acc_ref[rows_at(p * 16, 8), :], acc_ref[rows_at(p * 16 + 8, 8), :])
        one, two = run(ci[96 + p, 127] - HEAD, CHILD_TAIL, SLOTS - HEAD, chunk, start)
        sums[0, p] = one
        sums[1, p] = two
        return carry

    parts = []
    for i in range(4):
        lax.fori_loop(8 * i, 8 * i + 8, tail, 0)
        group = pl.ds(8 * i, 8)
        one, two = sums[0, group].reshape(64, 128), sums[1, group].reshape(64, 128)
        re, im = one - pltpu.roll(one, 64, 1), two + pltpu.roll(two, 64, 1)
        child[group, 0] = re[:, :64].reshape(8, 8, 64)
        child[group, 1] = im[:, :64].reshape(8, 8, 64)
        parts.append(pltpu.make_async_copy(child.at[group], child_out.at[group], sem.at[4 + i]))
        parts[i].start()
    pattern.wait()
    done.wait()
    for part in parts:
        part.wait()


def local(
    child_pattern, child_sources, child_classes, child_counts,
    parent_sources, parent_classes, parent_counts,
    child_table, parent_table, theta_index, theta_weight, phi_index, phi_weight, shift_angle,
):
    f32, i32 = jnp.float32, jnp.int32
    hbm = pl.BlockSpec(memory_space=pltpu.HBM)
    vmem = pl.BlockSpec(memory_space=pltpu.VMEM)
    dma = pltpu.SemaphoreType.DMA
    g, f, acc, pg, ci, pi = pl.pallas_call(
        gather_kernel,
        out_shape=(
            jax.ShapeDtypeStruct((4096, 128), f32),
            jax.ShapeDtypeStruct((6144, 128), f32),
            jax.ShapeDtypeStruct((512, 128), f32),
            jax.ShapeDtypeStruct((2080, 128), f32),
            pltpu.SMEM((128, 128), i32),
            pltpu.SMEM((32, 128), i32),
        ),
        in_specs=[hbm] * 13,
        out_specs=(vmem,) * 4 + (pl.BlockSpec(memory_space=pltpu.SMEM),) * 2,
        scratch_shapes=[
            pltpu.VMEM((32, 2, 8, 64), f32),
            pltpu.VMEM((SLOTS, 128), i32),
            pltpu.VMEM((SLOTS, 128), i32),
            pltpu.VMEM((4, 128), i32),
            pltpu.VMEM((8, SLOTS), i32),
            pltpu.VMEM((8, SLOTS), i32),
            pltpu.SMEM((64,), i32),
            pltpu.VMEM((2, 8, 64, CLASSES), f32),
            pltpu.VMEM((4, 128), i32),
            pltpu.VMEM((4, 128), f32),
            pltpu.VMEM((4, 16), i32),
            pltpu.VMEM((4, 16), f32),
            pltpu.VMEM((128, 128), f32),
            pltpu.VMEM((256, 128), f32),
            pltpu.VMEM((8, 2, 64, 128), f32),
            pltpu.VMEM((8, 2, 64, 128), f32),
            pltpu.VMEM((512, 128), f32),
            pltpu.VMEM((128, 256), f32),
            pltpu.VMEM((2, 128, 128), f32),
            pltpu.VMEM((80, 8, 128), f32),
            pltpu.VMEM((32, 128), i32),
            pltpu.VMEM((6, 128, 128), i32),
            pltpu.SMEM((32, 128), i32),
            pltpu.SMEM((32, 128), i32),
            dma((13,)),
            dma((7,)),
            dma((8, 2)),
            dma((8, 2)),
            dma((2, 4, CHUNKS)),
            dma((8, CHUNKS)),
            dma((8, CHUNKS)),
            dma((8, CHUNKS)),
            dma((8,)),
            dma((8,)),
        ],
        compiler_params=pltpu.CompilerParams(
            collective_id=0, has_side_effects=True, vmem_limit_bytes=24 * 2**20
        ),
        cost_estimate=pl.CostEstimate(flops=30_000_000_000, bytes_accessed=8_000_000, transcendentals=0),
        name="gather",
    )(*(pltpu.with_memory_space_constraint(x, pltpu.HBM) for x in (
        child_pattern,
        child_sources.T,
        child_classes.T,
        child_counts.reshape(4, 128),
        parent_sources,
        parent_classes,
        parent_counts,
        child_table.transpose(1, 2, 3, 0),
        theta_index.T,
        theta_weight.T,
        phi_index.T,
        phi_weight.T,
        shift_angle.reshape(128, 128),
    )))
    child_incoming, pattern, incoming = pl.pallas_call(
        list_kernel,
        out_shape=(
            jax.ShapeDtypeStruct((32, 2, 8, 64), f32),
            jax.ShapeDtypeStruct((128, 128), f32),
            jax.ShapeDtypeStruct((128, 128), f32),
        ),
        in_specs=[vmem] * 4 + [pl.BlockSpec(memory_space=pltpu.SMEM)] * 2 + [vmem],
        out_specs=(hbm, hbm, hbm),
        scratch_shapes=[
            pltpu.VMEM((32, 2, 8, 64), f32),
            pltpu.VMEM((128, 128), f32),
            pltpu.VMEM((2, 32, 8, 128), f32),
            dma((8,)),
        ],
        compiler_params=pltpu.CompilerParams(vmem_limit_bytes=24 * 2**20),
        name="lists",
    )(g, f, acc, pg, ci, pi, parent_table.reshape(CLASSES * 32, 128))
    shape = (4, 2, 16, 128)
    return child_incoming, pattern.reshape(shape), incoming.reshape(shape)


def solution(mesh):
    return jax.shard_map(
        local,
        mesh=mesh,
        in_specs=(
            P("clus", None, "ang", None),
            P(), P(), P(), P(), P(), P(),
            P(None, None, "ang", None),
            P(None, None, "ang", None),
            P(), P(),
            P("ang", None),
            P("ang", None),
            P(None, "ang", None),
        ),
        out_specs=(
            P("clus", None, "ang", None),
            P("clus", None, "ang", None),
            P("clus", None, "ang", None),
        ),
        check_vma=False,
    )
```
